128 devices in a mesh: brick: 16 (over z, y), gz: 8 (over x, core).
Axes of the slice: x: 4, y: 4, z: 4, core: 2. Of those that a mesh axis runs over, the one named last changes fastest.
Arguments:
- point_spots: float32 [8, 4096, 3, 128], P('gz', 'brick'), may hold values from 0 to 1
- point_values: float32 [8, 4096, 2, 128], P('gz', 'brick'), may hold values from -12 to 12
- dest_brick: int32 [8, 4096, 1], P('gz', 'brick'), may hold values from 0 to 15; in each aligned block of 256 rows (0 to 255, 256 to 511, ..., all dimensions but the last counted through in order) at most 24 rows name the same one
- dest_tile: int32 [8, 4096], P('gz', 'brick'), may hold values from 0 to 127
- live_count: int32 [8, 4096], P('gz', 'brick'), may hold values from 1 to 128, 393216 in all within a row
Outputs:
- density: float32 [2, 512, 512, 512], P(None, ('brick', 'gz'))
The draws below stay inside these ranges and needn't reach their ends.
Inputs may be any that keep to these rules, and one draw needn't show every extreme that they name: `dest_brick`: among the blocks of one device, at most 24 name the same brick, a bound that some block reaches of them.
All inputs are finite; a program needn't handle non-finite values. No bound on the sum of `live_count` on one device may be relied on, other than what follows from the above.
Results may differ from the reference program's by a relative error of at most 0.0043.
Values sent between devices are 32-bit elements; how exact they have to be, the bound alone decides.
No kernel may reach another device: no remote copies, remote signals or barrier semaphores. Data moves between devices by JAX's collectives and lax.ppermute only.
A program may use at most 128 MiB of HBM per device.

```python
import math
import jax
import jax.numpy as jnp
import numpy as np
from jax import lax

GRID = 512
TX = 16
TZ = 4
CAP = 128
BLK_DEV = 256
BLOCKS = 4096
SEND = 24
TILES_DEV = 128
N_BRICK = 16
N_GZ = 8


def set_ends(entries, own_key, smallest, largest):
    index_at = [jax.random.randint(jax.random.fold_in(own_key, axis), (), 0, length) for axis, length in enumerate(entries.shape)]
    main_axis = entries.shape.index(max(entries.shape))
    next_to = index_at[:main_axis] + [(index_at[main_axis] + 1) % entries.shape[main_axis]] + index_at[main_axis + 1:]
    return entries.at[tuple(index_at)].set(smallest).at[tuple(next_to)].set(largest)


def shard_levels(stream_key, dims, pieces, least, largest):
    gain = 1.0
    for dim, blocks in pieces:
        heights = jax.random.uniform(jax.random.fold_in(jax.random.fold_in(stream_key, 6), dim), (blocks,), jnp.float32, least / len(pieces), largest / len(pieces))
        gain = gain * jnp.repeat(jnp.exp(heights), dims[dim] // blocks).reshape((-1,) + (1,) * (len(dims) - 1 - dim))
    return gain


def profile(count, total, reach, slope):
    loads = [(1 << 20) // math.isqrt(standing ** slope) + 1 for standing in range(2, count + 1)]
    spare, counts = total - reach - (count - 1), [1] * (count - 1)
    while spare > 0:
        candidates = [i for i in range(count - 1) if counts[i] < reach]
        pool, left = sum([loads[i] for i in candidates]), spare
        for i in candidates:
            extra = min(reach - counts[i], max(1, left * loads[i] // pool), spare)
            counts[i] = counts[i] + extra
            spare = spare - extra
    return np.array([reach] + counts)


def uneven_parts(key, number_of, total, bound, skew):
    if number_of == 2:
        one = jax.random.randint(key, (), max(1, total - bound), min(bound, total - 1) + 1)
        return jnp.stack([one, total - one])
    tallies = jnp.asarray(profile(number_of, total, bound, skew), jnp.int32)
    pairs = (number_of - 1) // 2
    donor, receiver = tallies[1:1 + 2 * pairs:2], tallies[2:2 + 2 * pairs:2]
    margin = jnp.minimum(donor - 1, bound - receiver)
    moved = jax.random.randint(jax.random.fold_in(key, 1), (pairs,), 0, 1 << 20) % (margin + 1)
    tallies = tallies.at[1:1 + 2 * pairs:2].set(donor - moved).at[2:2 + 2 * pairs:2].set(receiver + moved)
    return tallies[jax.random.permutation(jax.random.fold_in(key, 2), number_of)]


def deal_out(key, own, number, rows, number_of, top, reach, slope):
    sequence = jax.random.permutation(key, number_of)
    crowded, usual = load_shares(number_of, rows * top, reach, slope, True), load_shares(number_of, rows * top, reach, slope, False)
    places = jnp.arange(number_of)

    def named(sizes, rotation):
        used = int((sizes > 0).sum())
        fixed = max(1, used // 4)
        moved = fixed + (places - fixed + rotation * (used - fixed)) % max(1, number_of - fixed)
        return jnp.zeros((number_of,), jnp.int32).at[sequence[jnp.where(places < fixed, places, moved)]].set(jnp.asarray(sizes, jnp.int32))

    sizes = jnp.where(number % 4 == 0, named(crowded, number // 4), named(usual, number - number // 4 - 1))
    mixed = jax.random.permutation(jax.random.fold_in(own, 3), number_of)
    giver, receiver = mixed[0:number_of // 2 * 2:2], mixed[1:number_of // 2 * 2:2]
    slack = jnp.minimum(sizes[giver] - 1, reach - sizes[receiver]) // 2
    slack = jnp.where((giver == sequence[0]) | (receiver == sequence[0]) | (sizes[receiver] == 0), 0, jnp.maximum(slack, 0))
    moved = jax.random.randint(jax.random.fold_in(own, 4), (number_of // 2,), 0, 1 << 20) % (slack + 1)
    sizes = sizes.at[giver].add(-moved).at[receiver].add(moved)
    members = jnp.searchsorted(jnp.cumsum(sizes), jnp.arange(rows * top), side="right").astype(jnp.int32)
    grid = members.reshape(top, rows).T
    grid = grid[jax.random.permutation(jax.random.fold_in(own, 1), rows)]
    rotation = jax.random.randint(jax.random.fold_in(own, 2), (rows, 1), 0, top)
    return jnp.take_along_axis(grid, (jnp.arange(top)[None, :] + rotation) % top, axis=1)


def load_shares(number_of, total, reach, skew, full):
    weights = [(1 << 20) // math.isqrt(grade ** skew) + 1 for grade in range(1, number_of + 1)]
    largest = reach if full else min(reach, max(-(-total // number_of), total * weights[0] // sum(weights)))
    least = 1 if total - largest >= number_of - 1 else 0
    counts, surplus = [largest] + [least] * (number_of - 1), total - largest - least * (number_of - 1)
    while surplus > 0:
        free = [i for i in range(1, number_of) if counts[i] < largest] or [i for i in range(1, number_of) if counts[i] < reach]
        mass, budget = sum([weights[i] for i in free]), surplus
        for i in free:
            addition = min(reach - counts[i], max(1, budget * weights[i] // mass), surplus)
            counts[i] = counts[i] + addition
            surplus = surplus - addition
    return np.array(counts)


def noise(key, dims, width, bound, split=(), held_as=jnp.bfloat16):
    gain = shard_levels(key, dims, split, -0.22, 0.18) if split else 1.0
    entries = jax.random.normal(key, dims, jnp.float32) * width * gain
    return jnp.minimum(jnp.maximum(entries, -bound), bound).astype(held_as)


def setup_inputs(seed: int = 0) -> dict:
    seeds = jax.random.split(jax.random.key(seed), 6)
    point_spots = jnp.clip(1.0 * jax.random.uniform(seeds[0], (N_GZ, BLOCKS, 3, CAP), jnp.float32) ** shard_levels(seeds[0], (N_GZ, BLOCKS, 3, CAP), ((0, 8), (1, 16)), -0.2, 0.2), 0.0, 1.0)
    point_values = noise(seeds[1], (N_GZ, BLOCKS, 2, CAP), 2.0, 12.0, ((0, 8), (1, 16)), jnp.float32)
    dest_brick_keys = jax.random.split(jax.random.fold_in(seeds[2], 1), N_GZ * BLOCKS // BLK_DEV)
    dest_brick_turns = jax.random.permutation(jax.random.fold_in(seeds[2], 3), N_GZ * BLOCKS // BLK_DEV)
    dest_brick = jax.vmap(lambda own, number: deal_out(jax.random.fold_in(seeds[2], 2), own, number, BLK_DEV, N_BRICK, 1, SEND, 2))(dest_brick_keys, dest_brick_turns).reshape((N_GZ, BLOCKS, 1))
    dest_tile = set_ends(jax.random.randint(seeds[3], (N_GZ, BLOCKS), 0, TILES_DEV), jax.random.fold_in(seeds[3], 1), 0, TILES_DEV - 1).astype(jnp.int32)
    live_count = jax.vmap(lambda own: uneven_parts(own, BLOCKS, BLOCKS * CAP * 3 // 4, CAP, 0))(jax.random.split(seeds[4], N_GZ)).reshape((N_GZ, BLOCKS)).astype(jnp.int32)
    return dict(point_spots=point_spots, point_values=point_values, dest_brick=dest_brick, dest_tile=dest_tile, live_count=live_count)


def kernel(spread_t):
    return jnp.maximum(0.0, 1.0 - spread_t * spread_t / 4.0) ** 10


def correction(length):
    places = jnp.arange(length, dtype=jnp.int32)
    shifted = jnp.where(places < length // 2, places, places - length)
    sample_nodes = jnp.arange(-63, 64, dtype=jnp.int32)
    phases = (shifted[:, None] * sample_nodes[None, :]).astype(jnp.float32) * (2.0 * math.pi / (32.0 * length))
    weights = kernel(sample_nodes.astype(jnp.float32) / 32.0)
    return jnp.sum(weights[None, :] * jnp.cos(phases), axis=1) / 32.0


def axis_weights(position, extent):
    offsets = jnp.arange(-1, 3, dtype=jnp.int32)
    cell_index = jnp.floor(position).astype(jnp.int32)[..., None] + offsets
    inside = (cell_index >= 0) & (cell_index < extent)
    weights = jnp.where(inside, kernel(cell_index.astype(jnp.float32) - position[..., None]), 0.0)
    return jnp.clip(cell_index, 0, extent - 1), weights


def reference(point_spots, point_values, dest_brick, dest_tile, live_count):
    brick_x = GRID // (N_BRICK // 4)
    brick_y = GRID // 4
    brick_z = GRID // N_GZ
    tiles_z = brick_z // TZ
    span_count = N_GZ * N_BRICK
    spot_rows = point_spots.reshape(span_count, BLK_DEV, 3, CAP)
    value_rows = point_values.reshape(span_count, BLK_DEV, 2, CAP)
    brick_rows = dest_brick.reshape(span_count, BLK_DEV)
    tile_rows = dest_tile.reshape(span_count, BLK_DEV)
    count_rows = live_count.reshape(span_count, BLK_DEV)

    def add_span(grid_sum, inputs):
        span, spots, values, target, tile, count = inputs
        slab_row = span // N_BRICK
        corner_x = (target // 4) * brick_x + (tile // tiles_z) * TX
        corner_y = (target % 4) * brick_y
        corner_z = slab_row * brick_z + (tile % tiles_z) * TZ
        cell_x, weight_x = axis_weights(-1.0 + (TX + 2) * spots[:, 0, :], TX)
        cell_y, weight_y = axis_weights(-1.0 + (brick_y + 2) * spots[:, 1, :], brick_y)
        cell_z, weight_z = axis_weights(-1.0 + (TZ + 2) * spots[:, 2, :], TZ)
        weight_x = lax.optimization_barrier(weight_x.astype(jnp.bfloat16)).astype(jnp.float32)
        live_mask = jnp.arange(CAP, dtype=jnp.int32)[None, :] < count[:, None]
        amplitude = jnp.where(live_mask[:, None, :], values, 0.0)
        yz_plane = weight_z[:, :, :, None] * weight_y[:, :, None, :]
        yz_terms = amplitude[:, :, :, None, None] * yz_plane[:, None]
        yz_terms = lax.optimization_barrier(yz_terms.astype(jnp.bfloat16)).astype(jnp.float32)
        contribution = weight_x[:, None, :, :, None, None] * yz_terms[:, :, :, None, :, :]
        global_x = corner_x[:, None, None] + cell_x
        global_y = corner_y[:, None, None] + cell_y
        global_z = corner_z[:, None, None] + cell_z
        flat_index = (global_x[:, :, :, None, None] * GRID + global_y[:, :, None, None, :]) * GRID + global_z[:, :, None, :, None]
        flat_index = jnp.broadcast_to(flat_index, contribution.shape[:1] + contribution.shape[2:]).reshape(-1)
        moved = jnp.moveaxis(contribution, 1, 0).reshape(2, -1)
        return grid_sum.at[:, flat_index].add(moved), None

    grid_sum = jnp.zeros((2, GRID * GRID * GRID), jnp.float32)
    grid_sum, _ = lax.scan(add_span, grid_sum, (jnp.arange(span_count, dtype=jnp.int32), spot_rows, value_rows, brick_rows, tile_rows, count_rows))
    spectrum = (grid_sum[0] + 1j * grid_sum[1]).reshape(GRID, GRID, GRID)
    density = jnp.fft.ifftn(spectrum) * (GRID ** 1.5)
    corrections = correction(GRID)
    density = density / (corrections[:, None, None] * corrections[None, :, None] * corrections[None, None, :])
    density = jnp.transpose(density, (2, 0, 1))
    return jnp.stack([jnp.real(density), jnp.imag(density)]).astype(jnp.float32)
```

```python
import functools
import math

import jax
import jax.numpy as jnp
import ml_dtypes
import numpy as np
from jax import lax
from jax.experimental import pallas as pl
from jax.experimental.pallas import tpu as pltpu
from jax.sharding import PartitionSpec as P

GRID = 512
TX = 16
TZ = 4
CAP = 128
AXES = ("brick", "gz")
PER_DEST = 24
ROWS1 = 5 * PER_DEST + 8
ROOM = 80
ROWS2 = 5 * ROOM + 8
LAST = 127
GROUP = 4
VMEM_LIMIT = 56 * 1024 * 1024


def correction_of(length):
    places = np.arange(length)
    shifted = np.where(places < length // 2, places, places - length)
    nodes = np.arange(-63, 64)
    weights = np.maximum(0.0, 1.0 - (nodes / 32.0) ** 2 / 4.0) ** 10
    phases = shifted[:, None] * nodes[None, :] * (2.0 * math.pi / (32.0 * length))
    return np.sum(weights[None, :] * np.cos(phases), axis=1) / 32.0


def split(table):
    high = table.astype(np.float32).astype(ml_dtypes.bfloat16)
    low = (table - high.astype(np.float64)).astype(np.float32).astype(ml_dtypes.bfloat16)
    return high, low


def quarter_tables(scale):
    k, b = np.arange(128)[:, None], np.arange(128)[None, :]
    out = []
    for r in range(4):
        turned = (b * (4 * k + r)) % GRID
        angle = turned * (2.0 * math.pi / GRID)
        gain = scale[4 * np.arange(128) + r][:, None]
        c, s = np.cos(angle) * gain, np.sin(angle) * gain
        out.append(np.block([[c, -s], [s, c]]))
    return split(np.stack(out))


def full_table(scale):
    y, k = np.arange(GRID)[:, None], np.arange(GRID)[None, :]
    angle = (y * k % GRID) * (2.0 * math.pi / GRID)
    c, s = np.cos(angle) * scale[None, :], np.sin(angle) * scale[None, :]
    return np.block([[c, s], [-s, c]]).astype(np.float32).astype(ml_dtypes.bfloat16)


def lanes():
    return lax.broadcasted_iota(jnp.int32, (1, CAP), 1)


def pack_bricks(brick_ref, tile_ref, live_ref, spots_ref, values_ref, out_ref, count_ref):
    lane = lanes()
    for b in range(16):
        count_ref[b] = 0
        out_ref[b * ROWS1 + 5 * PER_DEST : (b + 1) * ROWS1, :] = jnp.zeros((8, CAP), jnp.float32)

    def step(i, tally):
        b = brick_ref[i]
        r = count_ref[b]
        count_ref[b] = r + 1
        base = b * ROWS1
        for d in range(3):
            out_ref[pl.ds(base + d * PER_DEST + r, 1), :] = spots_ref[i, d : d + 1, :]
        live = lane < live_ref[i]
        for d in range(2):
            out_ref[pl.ds(base + (3 + d) * PER_DEST + r, 1), :] = jnp.where(
                live, values_ref[i, d : d + 1, :], 0.0
            )
        head = pl.ds(base + 5 * PER_DEST, 1)
        tile = tile_ref[i]
        out_ref[head, :] = jnp.where(lane == r, tile.astype(jnp.float32), out_ref[head, :])
        key = b * 8 + lax.shift_right_logical(tile, 4)
        return tally + jnp.where(lane == key, 1.0, 0.0)

    tally = lax.fori_loop(0, 256, step, jnp.zeros((1, CAP), jnp.float32), unroll=4)
    for b in range(16):
        row = b * ROWS1 + 5 * PER_DEST
        total = count_ref[b].astype(jnp.float32)
        out_ref[row : row + 1, :] = jnp.where(lane == LAST, total, out_ref[row : row + 1, :])
        out_ref[row + 1 : row + 2, :] = tally


def pack_tiles(round_ref, head_ref, data_ref, out_ref, count_ref):
    lane = lanes()
    first = round_ref[0] * ROOM
    for t in range(8):
        count_ref[t] = 0
        out_ref[t * ROWS2 + 5 * ROOM : (t + 1) * ROWS2, :] = jnp.zeros((8, CAP), jnp.float32)
    spare = 5 * ROOM + 7

    def source(s, carry):
        held = head_ref[s, LAST]

        def step(i, inner):
            tile = head_ref[s, i]
            live = i < held
            tx = lax.shift_right_logical(tile, 4)
            place = count_ref[tx]
            count_ref[tx] = place + live.astype(jnp.int32)
            k = place - first
            good = live & (k >= 0) & (k < ROOM)
            base = tx * ROWS2
            for d in range(5):
                row = jnp.where(good, base + d * ROOM + k, spare)
                out_ref[pl.ds(row, 1), :] = data_ref[pl.ds(s * ROWS1 + d * PER_DEST + i, 1), :]
            head = pl.ds(base + 5 * ROOM, 1)
            depth = (tile & 15).astype(jnp.float32)
            spot = jnp.where(good, k, -1)
            out_ref[head, :] = jnp.where(lane == spot, depth, out_ref[head, :])
            return inner

        return lax.fori_loop(0, PER_DEST, step, carry, unroll=4)

    lax.fori_loop(0, 16, source, 0)
    tally = data_ref[5 * PER_DEST + 1 : 5 * PER_DEST + 2, :]
    for s in range(1, 16):
        row = s * ROWS1 + 5 * PER_DEST + 1
        tally = tally + data_ref[row : row + 1, :]
    for t in range(8):
        row = t * ROWS2 + 5 * ROOM
        count = count_ref[t]
        sent = jnp.clip(count - first, 0, ROOM).astype(jnp.float32)
        out_ref[row : row + 1, :] = jnp.where(lane == LAST, sent, out_ref[row : row + 1, :])
        out_ref[row + 1 : row + 2, :] = tally


def phi10(t):
    square = t * t
    fourth = square * square
    return fourth * fourth * square


def weights_at(cells, position):
    half = cells - 0.5 * position
    return phi10(jnp.maximum(0.0, 1.0 - half * half))


def halves(value):
    high = value.astype(jnp.bfloat16)
    return high, (value - high.astype(jnp.float32)).astype(jnp.bfloat16)


def block_cells(data_ref, row, scale):
    def at(d):
        return data_ref[pl.ds(row + d * ROOM, 1), :]

    pos_x = -1.0 + (TX + 2) * at(0)
    pos_y = -1.0 + (CAP + 2) * at(1)
    pos_z = -1.0 + (TZ + 2) * at(2)
    half_cells = 0.5 * lax.broadcasted_iota(jnp.int32, (CAP, CAP), 0).astype(jnp.float32)
    wy = weights_at(half_cells, pos_y)
    wx = weights_at(half_cells[:TX], pos_x).astype(jnp.bfloat16).astype(jnp.float32)
    wz = weights_at(half_cells[:8], pos_z)
    parts = []
    for d in (3, 4):
        wzv = wz * (at(d) * scale)
        for l in range(TZ):
            parts.append(wx * wzv[l : l + 1, :])
    left = jnp.concatenate(parts, axis=0)
    left_high, left_low = halves(left)
    high, low = halves(wy)
    return lax.dot_general(
        jnp.concatenate([left_high, left_high, left_low], axis=1),
        jnp.concatenate([high, low, high], axis=1),
        (((1,), (1,)), ((), ())),
        preferred_element_type=jnp.float32,
    )


def add_blocks(head_ref, data_ref, grid_ref):
    for g in range(8):
        held = head_ref[g, LAST]

        def group(n, carry, g=g, held=held):
            found = []
            for u in range(GROUP):
                i = n * GROUP + u
                live = i < held
                i = jnp.where(live, i, 0)
                scale = jnp.where(live, 1.0, 0.0).astype(jnp.float32)
                tile = head_ref[g, i] + 16 * g
                found.append((tile, block_cells(data_ref, g * ROWS2 + i, scale)))
            for tile, cells in found:
                for a in range(2):
                    rows = pl.ds(pl.multiple_of(a * 8192 + tile * 64, 64), 64)
                    grid_ref[rows, :] += cells[a * 64 : (a + 1) * 64]
            return carry

        lax.fori_loop(0, (held + GROUP - 1) // GROUP, group, 0)


def start_grid(flag_ref, extra_ref, grid_ref, sem):
    @pl.when(flag_ref[0] > 0)
    def _():
        copy = pltpu.make_async_copy(extra_ref, grid_ref, sem)
        copy.start()
        copy.wait()

    @pl.when(flag_ref[0] <= 0)
    def _():
        def clear(i, carry):
            grid_ref[pl.ds(pl.multiple_of(i * 64, 64), 64), :] = jnp.zeros((64, CAP), jnp.float32)
            return carry

        lax.fori_loop(0, 16384 // 64, clear, 0, unroll=4)


def spread_only(flag_ref, head_ref, data_ref, extra_ref, grid_ref, sem):
    start_grid(flag_ref, extra_ref, grid_ref, sem)
    add_blocks(head_ref, data_ref, grid_ref)


def quarters(re, im):
    s02r, s02i = re[0] + re[2], im[0] + im[2]
    d02r, d02i = re[0] - re[2], im[0] - im[2]
    s13r, s13i = re[1] + re[3], im[1] + im[3]
    d13r, d13i = re[1] - re[3], im[1] - im[3]
    return [
        (s02r + s13r, s02i + s13i),
        (d02r - d13i, d02i + d13r),
        (s02r - s13r, s02i - s13i),
        (d02r + d13i, d02i - d13r),
    ]


def three_pass(high, low, value):
    top, rest = halves(value)

    def dot(a, b):
        return jnp.dot(a, b, preferred_element_type=jnp.float32)

    return dot(high, top) + (dot(high, rest) + dot(low, top))


def spread_and_turn(
    flag_ref, head_ref, data_ref, high_ref, low_ref, extra_ref, out_ref, grid_ref, sem
):
    start_grid(flag_ref, extra_ref, grid_ref, sem)
    add_blocks(head_ref, data_ref, grid_ref)

    def columns(n, carry):
        j = 2 * n

        def plane(a, q):
            return jnp.concatenate(
                [
                    grid_ref[pl.ds(a * 8192 + q * 2048 + j + u, 128, stride=16), :]
                    for u in range(2)
                ],
                axis=1,
            )

        re = [plane(0, q) for q in range(4)]
        im = [plane(1, q) for q in range(4)]
        for r, (real, imag) in enumerate(quarters(re, im)):
            turned = three_pass(high_ref[r], low_ref[r], jnp.concatenate([real, imag], axis=0))
            for a in range(2):
                for u in range(2):
                    out_ref[pl.ds(r * 32 + a * 16 + j + u, 128, stride=128), :] = turned[
                        a * 128 : (a + 1) * 128, u * 128 : (u + 1) * 128
                    ]
        return carry

    lax.fori_loop(0, 8, columns, 0)


def turn_planes(data_ref, high_ref, low_ref, y_ref, out_ref, rows_ref, left_ref):
    def plane(c, bx, by):
        return data_ref[bx, by, :, 0, c].reshape(128, CAP)

    for pair in range(2):
        ys = (2 * pair, 2 * pair + 1)
        re = [jnp.concatenate([plane(0, bx, by) for by in ys], axis=1) for bx in range(4)]
        im = [jnp.concatenate([plane(1, bx, by) for by in ys], axis=1) for bx in range(4)]
        for r, (real, imag) in enumerate(quarters(re, im)):
            turned = three_pass(high_ref[r], low_ref[r], jnp.concatenate([real, imag], axis=0))
            for a in range(2):
                for u in range(2):
                    start = (a * 4 + ys[u]) * GRID + r
                    rows_ref[pl.ds(start, 128, stride=4), :] = turned[
                        a * 128 : (a + 1) * 128, u * 128 : (u + 1) * 128
                    ]
    for n in range(8):
        left_ref[:, n * 128 : (n + 1) * 128] = rows_ref[n * GRID : (n + 1) * GRID, :].astype(
            jnp.bfloat16
        )
    for n in range(4):
        out_ref[n // 2, 0, :, (n % 2) * 256 : (n % 2 + 1) * 256] = jnp.dot(
            left_ref[...], y_ref[:, n * 256 : (n + 1) * 256], preferred_element_type=jnp.float32
        )


def smem():
    return pl.BlockSpec(memory_space=pltpu.SMEM)


def vmem():
    return pl.BlockSpec(memory_space=pltpu.VMEM)


def params():
    return pltpu.CompilerParams(vmem_limit_bytes=VMEM_LIMIT)


def swap(array, axis):
    return lax.all_to_all(array, axis, split_axis=0, concat_axis=0, tiled=True)


def body(z_high, z_low, x_high, x_low, y_table, spots, values, dest_brick, dest_tile, live_count):
    f32 = jnp.float32
    sent = pl.pallas_call(
        pack_bricks,
        out_shape=jax.ShapeDtypeStruct((16 * ROWS1, CAP), f32),
        in_specs=[smem(), smem(), smem(), vmem(), vmem()],
        out_specs=vmem(),
        scratch_shapes=[pltpu.SMEM((16,), jnp.int32)],
        compiler_params=params(),
        name="pack_bricks",
    )(dest_brick.reshape(256), dest_tile[0], live_count[0], spots[0], values[0])
    held = swap(sent.reshape(16, ROWS1, CAP), "brick")
    head = held[:, 5 * PER_DEST].astype(jnp.int32)
    held = held.reshape(16 * ROWS1, CAP)

    def exchange(turn):
        packed = pl.pallas_call(
            pack_tiles,
            out_shape=jax.ShapeDtypeStruct((8 * ROWS2, CAP), f32),
            in_specs=[smem(), smem(), vmem()],
            out_specs=vmem(),
            scratch_shapes=[pltpu.SMEM((8,), jnp.int32)],
            compiler_params=params(),
            name="pack_tiles",
        )(turn, head, held)
        blocks = swap(packed.reshape(8, ROWS2, CAP), "gz")
        return blocks.reshape(8 * ROWS2, CAP), blocks[:, 5 * ROOM : 5 * ROOM + 2].astype(jnp.int32)

    blocks, heads = exchange(jnp.zeros((1,), jnp.int32))
    tiles = heads[:, 0]
    rounds = ((jnp.max(heads[:, 1]) + ROOM - 1) // ROOM).reshape(1)

    nothing = pl.pallas_call(
        lambda out_ref: None,
        out_shape=jax.ShapeDtypeStruct((16384, CAP), f32),
        out_specs=pl.BlockSpec(memory_space=pl.ANY),
        name="nothing",
    )()

    def more(state):
        return state[0][0] < rounds[0]

    def another(state):
        turn, extra = state
        part, part_heads = exchange(turn)
        extra = pl.pallas_call(
            spread_only,
            out_shape=jax.ShapeDtypeStruct((16384, CAP), f32),
            in_specs=[smem(), smem(), vmem(), pl.BlockSpec(memory_space=pl.ANY)],
            out_specs=vmem(),
            scratch_shapes=[pltpu.SemaphoreType.DMA],
            compiler_params=params(),
            name="spread_only",
        )(turn - 1, part_heads[:, 0], part, extra)
        return turn + 1, extra

    _, extra = lax.while_loop(more, another, (jnp.ones((1,), jnp.int32), nothing))

    columns = pl.pallas_call(
        spread_and_turn,
        out_shape=jax.ShapeDtypeStruct((16384, CAP), f32),
        in_specs=[smem(), smem(), vmem(), vmem(), vmem(), pl.BlockSpec(memory_space=pl.ANY)],
        out_specs=vmem(),
        scratch_shapes=[pltpu.VMEM((16384, CAP), f32), pltpu.SemaphoreType.DMA],
        compiler_params=params(),
        name="spread_and_turn",
    )(rounds - 1, tiles, blocks, z_high, z_low, extra)
    planes = swap(columns.reshape(128, 4, 2, TX, CAP), AXES).reshape(4, 4, 8, 4, 2, TX, CAP)
    return pl.pallas_call(
        turn_planes,
        grid=(4,),
        out_shape=jax.ShapeDtypeStruct((2, 4, GRID, GRID), f32),
        in_specs=[
            pl.BlockSpec((4, 4, 8, 1, 2, TX, CAP), lambda q: (0, 0, 0, q, 0, 0, 0)),
            vmem(),
            vmem(),
            vmem(),
        ],
        out_specs=pl.BlockSpec((2, 1, GRID, GRID), lambda q: (0, q, 0, 0)),
        scratch_shapes=[
            pltpu.VMEM((8 * GRID, CAP), f32),
            pltpu.VMEM((GRID, 2 * GRID), jnp.bfloat16),
        ],
        compiler_params=params(),
        name="turn_planes",
    )(planes, x_high, x_low, y_table)


def solution(mesh):
    in_specs = (
        P("gz", "brick", None, None),
        P("gz", "brick", None, None),
        P("gz", "brick", None),
        P("gz", "brick"),
        P("gz", "brick"),
    )
    out_specs = P(None, AXES, None, None)
    inverse = 1.0 / correction_of(GRID)
    z_high, z_low = quarter_tables(inverse * GRID ** (-1.5))
    x_high, x_low = quarter_tables(inverse)
    y_table = full_table(inverse)

    def whole(*args):
        tables = [jnp.asarray(t) for t in (z_high, z_low, x_high, x_low, y_table)]
        return jax.shard_map(
            functools.partial(body),
            mesh=mesh,
            in_specs=(P(),) * 5 + in_specs,
            out_specs=out_specs,
            check_vma=False,
        )(*tables, *args)

    return whole
```

```python
import functools
import math

import jax
import jax.numpy as jnp
import ml_dtypes
import numpy as np
from jax import lax
from jax.experimental import pallas as pl
from jax.experimental.pallas import tpu as pltpu
from jax.sharding import PartitionSpec as P

GRID = 512
TX = 16
TZ = 4
CAP = 128
AXES = ("brick", "gz")
PER_DEST = 24
ROWS1 = 5 * PER_DEST + 8
ROOM = 80
ROWS2 = 5 * ROOM + 8
LAST = 127
SLOTS = 3
STRAYS = 32
ROWS_S = 5 * STRAYS + 8
MARK = 1e30
GROUP = 16
DEPTH = 24
WIDE = 136
VMEM_LIMIT = 56 * 1024 * 1024


def correction_of(length):
    places = np.arange(length)
    shifted = np.where(places < length // 2, places, places - length)
    nodes = np.arange(-63, 64)
    weights = np.maximum(0.0, 1.0 - (nodes / 32.0) ** 2 / 4.0) ** 10
    phases = shifted[:, None] * nodes[None, :] * (2.0 * math.pi / (32.0 * length))
    return np.sum(weights[None, :] * np.cos(phases), axis=1) / 32.0


def split(table):
    high = table.astype(np.float32).astype(ml_dtypes.bfloat16)
    low = (table - high.astype(np.float64)).astype(np.float32).astype(ml_dtypes.bfloat16)
    return high, low


def quarter_tables(scale):
    k, b = np.arange(128)[:, None], np.arange(128)[None, :]
    out = []
    for r in range(4):
        turned = (b * (4 * k + r)) % GRID
        angle = turned * (2.0 * math.pi / GRID)
        gain = scale[4 * np.arange(128) + r][:, None]
        c, s = np.cos(angle) * gain, np.sin(angle) * gain
        out.append(np.block([[c, -s], [s, c]]))
    return split(np.stack(out))


def full_table(scale):
    y, k = np.arange(GRID)[:, None], np.arange(GRID)[None, :]
    angle = (y * k % GRID) * (2.0 * math.pi / GRID)
    c, s = np.cos(angle) * scale[None, :], np.sin(angle) * scale[None, :]
    return np.block([[c, s], [-s, c]]).astype(np.float32).astype(ml_dtypes.bfloat16)


def lanes():
    return lax.broadcasted_iota(jnp.int32, (1, CAP), 1)


def pack_blocks(
    me_ref, brick_ref, tile_ref, live_ref, spots_ref, values_ref, out_ref,
    place_ref, left_ref, count_ref, turn_ref,
):
    lane = lanes()

    def clear(k, carry):
        count_ref[k] = 0
        out_ref[pl.ds(k * 16 + 15, 1), :] = jnp.full((1, CAP), -1.0, jnp.float32)
        return carry

    lax.fori_loop(0, 128, clear, 0, unroll=8)
    for b in range(16):
        turn_ref[b] = me_ref[0]

    def direct(i, left):
        key = brick_ref[i] * 8 + lax.shift_right_logical(tile_ref[i], 4)
        count = count_ref[key]
        place_ref[i] = key * 16 + count
        count_ref[key] = jnp.minimum(count + 1, SLOTS)
        left_ref[left] = i
        return left + (count >= SLOTS).astype(jnp.int32)

    strays = lax.fori_loop(0, 256, direct, 0, unroll=4)

    def stray(n, carry):
        i = left_ref[n]
        b = brick_ref[i]
        turn = lax.while_loop(
            lambda p: count_ref[b * 8 + (p & 7)] >= SLOTS, lambda p: p + 1, turn_ref[b]
        )
        key = b * 8 + (turn & 7)
        place_ref[i] = key * 16 + count_ref[key]
        count_ref[key] = count_ref[key] + 1
        turn_ref[b] = turn
        return carry

    lax.fori_loop(0, strays, stray, 0)

    def move(i, carry):
        row = place_ref[i]
        slot = row & 15
        for d in range(3):
            out_ref[pl.ds(row + d * SLOTS, 1), :] = spots_ref[d, pl.ds(i, 1), :]
        live = lane < live_ref[i]
        for d in range(2):
            out_ref[pl.ds(row + (3 + d) * SLOTS, 1), :] = jnp.where(
                live, values_ref[i, d : d + 1, :], 0.0
            )
        head = pl.ds(row - slot + 15, 1)
        out_ref[head, :] = jnp.where(lane == slot, tile_ref[i].astype(jnp.float32), out_ref[head, :])
        return carry

    lax.fori_loop(0, 256, move, 0, unroll=8)


def sort_blocks(
    me_ref, head_ref, data_ref, out_ref, row_ref, tile_ref, note_ref, left_ref, count_ref
):
    lane = lanes()
    me = me_ref[0]
    for t in range(8):
        count_ref[t] = 0
        out_ref[t * ROWS_S + 5 * STRAYS : (t + 1) * ROWS_S, :] = jnp.zeros((8, CAP), jnp.float32)

    def look(source, found):
        own, strays = found
        for c in range(SLOTS):
            tile = head_ref[source * SLOTS + c]
            tx = lax.shift_right_arithmetic(tile, 4)
            straight = (tx == me).astype(jnp.int32)
            row_ref[own] = source * 16 + c
            tile_ref[own] = (source & 7) * 16 + (tile & 15)
            own = own + straight
            left_ref[strays] = source * SLOTS + c
            strays = strays + (tile >= 0).astype(jnp.int32) - straight
        return own, strays

    own, strays = lax.fori_loop(0, 128, look, (0, 0), unroll=2)

    def forward(n, carry):
        entry = left_ref[n]
        source = entry // SLOTS
        row = source * 16 + entry - source * SLOTS
        tile = head_ref[entry]
        tx = lax.shift_right_logical(tile, 4)
        k = count_ref[tx]
        count_ref[tx] = k + 1
        k = jnp.minimum(k, STRAYS - 1)
        for d in range(5):
            out_ref[pl.ds(tx * ROWS_S + d * STRAYS + k, 1), :] = data_ref[
                pl.ds(row + d * SLOTS, 1), :
            ]
        head = pl.ds(tx * ROWS_S + 5 * STRAYS, 1)
        depth = ((source & 7) * 16 + (tile & 15)).astype(jnp.float32)
        out_ref[head, :] = jnp.where(lane == k, depth, out_ref[head, :])
        return carry

    lax.fori_loop(0, strays, forward, 0)
    most = count_ref[0]
    for t in range(8):
        row = t * ROWS_S + 5 * STRAYS
        count = count_ref[t]
        most = jnp.maximum(most, count)
        sent = jnp.minimum(count, STRAYS).astype(jnp.float32)
        out_ref[row : row + 1, :] = jnp.where(lane == LAST, sent, out_ref[row : row + 1, :])
    note_ref[0] = own
    note_ref[1] = (most > STRAYS).astype(jnp.int32)


def pack_bricks(brick_ref, tile_ref, live_ref, spots_ref, values_ref, out_ref, count_ref):
    lane = lanes()
    for b in range(16):
        count_ref[b] = 0
        out_ref[b * ROWS1 + 5 * PER_DEST : (b + 1) * ROWS1, :] = jnp.zeros((8, CAP), jnp.float32)

    def step(i, tally):
        b = brick_ref[i]
        r = count_ref[b]
        count_ref[b] = r + 1
        base = b * ROWS1
        for d in range(3):
            out_ref[pl.ds(base + d * PER_DEST + r, 1), :] = spots_ref[d, pl.ds(i, 1), :]
        live = lane < live_ref[i]
        for d in range(2):
            out_ref[pl.ds(base + (3 + d) * PER_DEST + r, 1), :] = jnp.where(
                live, values_ref[i, d : d + 1, :], 0.0
            )
        head = pl.ds(base + 5 * PER_DEST, 1)
        tile = tile_ref[i]
        out_ref[head, :] = jnp.where(lane == r, tile.astype(jnp.float32), out_ref[head, :])
        key = b * 8 + lax.shift_right_logical(tile, 4)
        return tally + jnp.where(lane == key, 1.0, 0.0)

    tally = lax.fori_loop(0, 256, step, jnp.zeros((1, CAP), jnp.float32), unroll=4)
    for b in range(16):
        row = b * ROWS1 + 5 * PER_DEST
        total = count_ref[b].astype(jnp.float32)
        out_ref[row : row + 1, :] = jnp.where(lane == LAST, total, out_ref[row : row + 1, :])
        out_ref[row + 1 : row + 2, :] = tally


def pack_tiles(round_ref, head_ref, data_ref, out_ref, count_ref):
    lane = lanes()
    first = round_ref[0] * ROOM
    for t in range(8):
        count_ref[t] = 0
        out_ref[t * ROWS2 + 5 * ROOM : (t + 1) * ROWS2, :] = jnp.zeros((8, CAP), jnp.float32)
    spare = 5 * ROOM + 7

    def source(s, carry):
        held = head_ref[s, LAST]

        def step(i, inner):
            tile = head_ref[s, i]
            live = i < held
            tx = lax.shift_right_logical(tile, 4)
            place = count_ref[tx]
            count_ref[tx] = place + live.astype(jnp.int32)
            k = place - first
            good = live & (k >= 0) & (k < ROOM)
            base = tx * ROWS2
            for d in range(5):
                row = jnp.where(good, base + d * ROOM + k, spare)
                out_ref[pl.ds(row, 1), :] = data_ref[pl.ds(s * ROWS1 + d * PER_DEST + i, 1), :]
            head = pl.ds(base + 5 * ROOM, 1)
            depth = (tile & 15).astype(jnp.float32)
            spot = jnp.where(good, k, -1)
            out_ref[head, :] = jnp.where(lane == spot, depth, out_ref[head, :])
            return inner

        return lax.fori_loop(0, PER_DEST, step, carry, unroll=4)

    lax.fori_loop(0, 16, source, 0)
    tally = data_ref[5 * PER_DEST + 1 : 5 * PER_DEST + 2, :]
    for s in range(1, 16):
        row = s * ROWS1 + 5 * PER_DEST + 1
        tally = tally + data_ref[row : row + 1, :]
    for t in range(8):
        row = t * ROWS2 + 5 * ROOM
        count = count_ref[t]
        sent = jnp.clip(count - first, 0, ROOM).astype(jnp.float32)
        out_ref[row : row + 1, :] = jnp.where(lane == LAST, sent, out_ref[row : row + 1, :])
        out_ref[row + 1 : row + 2, :] = tally


def phi10(t):
    square = t * t
    fourth = square * square
    return fourth * fourth * square


def weights_at(cells, position):
    half = cells - 0.5 * position
    return phi10(jnp.maximum(0.0, 1.0 - half * half))


def halves(value):
    high = value.astype(jnp.bfloat16)
    return high, (value - high.astype(jnp.float32)).astype(jnp.bfloat16)


def block_cells(data_ref, row, step, scale):
    def at(d):
        return data_ref[pl.ds(row + d * step, 1), :]

    pos_x = -1.0 + (TX + 2) * at(0)
    pos_y = -1.0 + (CAP + 2) * at(1)
    pos_z = -1.0 + (TZ + 2) * at(2)
    half_cells = 0.5 * lax.broadcasted_iota(jnp.int32, (TX, CAP), 0).astype(jnp.float32)
    wx = weights_at(half_cells, pos_x).astype(jnp.bfloat16).astype(jnp.float32)
    wz = weights_at(half_cells[:8], pos_z)
    parts = []
    for d in (3, 4):
        wzv = wz * (at(d) * scale)
        for l in range(TZ):
            parts.append(wx * wzv[l : l + 1, :])
    left_high, left_low = halves(jnp.concatenate(parts, axis=0))
    first = jnp.floor(pos_y) - 1.0
    near_high, near_low = halves(weights_at(half_cells[:8], pos_y - first))
    cells = lax.broadcasted_iota(jnp.int32, (CAP, CAP), 0).astype(jnp.float32)
    place = cells.astype(jnp.bfloat16) - first.astype(jnp.bfloat16)
    high = jnp.zeros((CAP, CAP), jnp.bfloat16)
    low = high
    for k in range(4):
        here = place == jnp.bfloat16(k)
        high = jnp.where(here, near_high[k : k + 1, :], high)
        low = jnp.where(here, near_low[k : k + 1, :], low)
    return lax.dot_general(
        jnp.concatenate([left_high, left_high, left_low], axis=1),
        jnp.concatenate([high, low, high], axis=1),
        (((1,), (1,)), ((), ())),
        preferred_element_type=jnp.float32,
    )


def add_listed(row_ref, tile_ref, held, step, data_ref, grid_ref, depth):
    def group(n, carry):
        found = []
        for u in range(GROUP):
            i = n * GROUP + u
            live = i < held
            i = jnp.where(live, i, 0)
            scale = jnp.where(live, 1.0, 0.0).astype(jnp.float32)
            found.append((tile_ref[i], block_cells(data_ref, row_ref[i], step, scale)))
        for tile, cells in found:
            for a in range(2):
                for l in range(TZ):
                    start = (a * 512 + tile * TZ + l) * depth
                    rows = pl.ds(pl.multiple_of(start, 8), TX)
                    part = (a * TZ + l) * TX
                    grid_ref[rows, :] += cells[part : part + TX]
        return carry

    lax.fori_loop(0, (held + GROUP - 1) // GROUP, group, 0)


def list_headed(head_ref, row_ref, tile_ref, room, base):
    def source(g, total):
        def entry(i, at):
            row_ref[at] = g * (5 * room + 8) + i
            tile_ref[at] = head_ref[g, i] + base * g
            return at + 1

        return lax.fori_loop(0, head_ref[g, LAST], entry, total)

    return lax.fori_loop(0, 8, source, 0)


def clear_grid(grid_ref):
    def clear(i, carry):
        grid_ref[pl.ds(pl.multiple_of(i * 64, 64), 64), :] = jnp.zeros((64, CAP), jnp.float32)
        return carry

    lax.fori_loop(0, 16384 // 64, clear, 0, unroll=4)


def spread_direct(note_ref, row_ref, tile_ref, data_ref, grid_ref):
    clear_grid(grid_ref)
    add_listed(row_ref, tile_ref, note_ref[0], SLOTS, data_ref, grid_ref, TX)


def spread_round(head_ref, data_ref, from_ref, grid_ref, row_ref, tile_ref, sem):
    copy = pltpu.make_async_copy(from_ref, grid_ref, sem)
    copy.start()
    copy.wait()
    held = list_headed(head_ref, row_ref, tile_ref, ROOM, 16)
    add_listed(row_ref, tile_ref, held, ROOM, data_ref, grid_ref, TX)


def quarters(re, im):
    s02r, s02i = re[0] + re[2], im[0] + im[2]
    d02r, d02i = re[0] - re[2], im[0] - im[2]
    s13r, s13i = re[1] + re[3], im[1] + im[3]
    d13r, d13i = re[1] - re[3], im[1] - im[3]
    return [
        (s02r + s13r, s02i + s13i),
        (d02r - d13i, d02i + d13r),
        (s02r - s13r, s02i - s13i),
        (d02r + d13i, d02i - d13r),
    ]


def three_pass(high, low, value):
    top, rest = halves(value)

    def dot(a, b):
        return jnp.dot(a, b, preferred_element_type=jnp.float32)

    return dot(high, top) + (dot(high, rest) + dot(low, top))


def spread_and_turn(
    note_ref, head_ref, data_ref, high_ref, low_ref, from_ref, out_ref,
    grid_ref, sent_ref, row_ref, tile_ref, sem, out_sem,
):
    copy = pltpu.make_async_copy(from_ref, grid_ref.at[:, pl.ds(0, TX), :], sem)
    copy.start()
    held = list_headed(head_ref, row_ref, tile_ref, STRAYS, 0)
    copy.wait()
    flat = grid_ref.reshape(1024 * DEPTH, CAP)
    sent = sent_ref.reshape(128 * WIDE, CAP)
    add_listed(row_ref, tile_ref, held, STRAYS, data_ref, flat, DEPTH)

    def columns(n, carry):
        j = 2 * n

        def plane(a, q):
            return jnp.concatenate(
                [
                    flat[pl.ds((a * 512 + q * 128) * DEPTH + j + u, 128, stride=DEPTH), :]
                    for u in range(2)
                ],
                axis=1,
            )

        re = [plane(0, q) for q in range(4)]
        im = [plane(1, q) for q in range(4)]
        for r, (real, imag) in enumerate(quarters(re, im)):
            turned = three_pass(high_ref[r], low_ref[r], jnp.concatenate([real, imag], axis=0))
            for a in range(2):
                for u in range(2):
                    sent[pl.ds(r * 32 + a * 16 + j + u, 128, stride=WIDE), :] = turned[
                        a * 128 : (a + 1) * 128, u * 128 : (u + 1) * 128
                    ]
        return carry

    def outward(n):
        return pltpu.make_async_copy(sent_ref.at[:, n], out_ref.at[:, n], out_sem.at[n])

    lax.fori_loop(0, 4, columns, 0)

    @pl.when(note_ref[1] > 0)
    def _():
        sent[pl.ds(0, 128, stride=WIDE), :] = jnp.full((128, CAP), MARK, jnp.float32)

    for n in range(8):
        outward(2 * n).start()
    lax.fori_loop(4, 8, columns, 0)
    for n in range(8):
        outward(2 * n + 1).start()
    for n in range(16):
        outward(n).wait()


def turn_planes(data_ref, high_ref, low_ref, y_ref, out_ref, mark_ref, rows_ref, left_ref):
    @pl.when(pl.program_id(0) == 0)
    def _():
        most = data_ref[0, 0, :, 0, 0, 0]
        for n in range(1, 16):
            most = jnp.maximum(most, data_ref[n // 4, n % 4, :, 0, 0, 0])
        mark_ref[0] = (jnp.max(most) > 0.1 * MARK).astype(jnp.int32)

    def plane(c, bx, by):
        return data_ref[bx, by, :, 0, c].reshape(128, CAP)

    for pair in range(2):
        ys = (2 * pair, 2 * pair + 1)
        re = [jnp.concatenate([plane(0, bx, by) for by in ys], axis=1) for bx in range(4)]
        im = [jnp.concatenate([plane(1, bx, by) for by in ys], axis=1) for bx in range(4)]
        for r, (real, imag) in enumerate(quarters(re, im)):
            turned = three_pass(high_ref[r], low_ref[r], jnp.concatenate([real, imag], axis=0))
            for a in range(2):
                for u in range(2):
                    start = (a * 4 + ys[u]) * GRID + r
                    rows_ref[pl.ds(start, 128, stride=4), :] = turned[
                        a * 128 : (a + 1) * 128, u * 128 : (u + 1) * 128
                    ]
    for n in range(8):
        left_ref[:, n * 128 : (n + 1) * 128] = rows_ref[n * GRID : (n + 1) * GRID, :].astype(
            jnp.bfloat16
        )
    for n in range(4):
        out_ref[n // 2, 0, :, (n % 2) * 256 : (n % 2 + 1) * 256] = jnp.dot(
            left_ref[...], y_ref[:, n * 256 : (n + 1) * 256], preferred_element_type=jnp.float32
        )


def smem():
    return pl.BlockSpec(memory_space=pltpu.SMEM)


def vmem():
    return pl.BlockSpec(memory_space=pltpu.VMEM)


def params():
    return pltpu.CompilerParams(vmem_limit_bytes=VMEM_LIMIT)


def swap(array, axis):
    return lax.all_to_all(array, axis, split_axis=0, concat_axis=0, tiled=True)


def call(kernel, out_shape, in_specs, out_specs, **options):
    return pl.pallas_call(
        kernel,
        out_shape=out_shape,
        in_specs=in_specs,
        out_specs=out_specs,
        compiler_params=params(),
        name=kernel.__name__,
        **options,
    )


def anywhere():
    return pl.BlockSpec(memory_space=pl.ANY)


def rows_of(rows):
    return jax.ShapeDtypeStruct((rows, CAP), jnp.float32)


def ints(count):
    return jax.ShapeDtypeStruct((count,), jnp.int32)


def body(z_high, z_low, x_high, x_low, y_table, spots, values, dest_brick, dest_tile, live_count):
    points = (
        dest_brick.reshape(256),
        dest_tile[0],
        live_count[0],
        spots[0].transpose(1, 0, 2),
        values[0],
    )

    def finish(note, heads, data, grid):
        columns = call(
            spread_and_turn,
            jax.ShapeDtypeStruct((128, 16, 8, CAP), jnp.float32),
            [smem(), smem(), vmem(), vmem(), vmem(), anywhere()],
            anywhere(),
            scratch_shapes=[
                pltpu.VMEM((1024, DEPTH, CAP), jnp.float32),
                pltpu.VMEM((128, WIDE // 8, 8, CAP), jnp.float32),
                pltpu.SMEM((8 * STRAYS,), jnp.int32),
                pltpu.SMEM((8 * STRAYS,), jnp.int32),
                pltpu.SemaphoreType.DMA,
                pltpu.SemaphoreType.DMA((16,)),
            ],
        )(note, heads, data, z_high, z_low, grid.reshape(1024, TX, CAP))
        planes = swap(columns.reshape(128, 4, 2, TX, CAP), AXES).reshape(4, 4, 8, 4, 2, TX, CAP)
        return call(
            turn_planes,
            (jax.ShapeDtypeStruct((2, 4, GRID, GRID), jnp.float32), ints(1)),
            [
                pl.BlockSpec((4, 4, 8, 1, 2, TX, CAP), lambda q: (0, 0, 0, q, 0, 0, 0)),
                vmem(),
                vmem(),
                vmem(),
            ],
            (pl.BlockSpec((2, 1, GRID, GRID), lambda q: (0, q, 0, 0)), smem()),
            grid=(4,),
            scratch_shapes=[
                pltpu.VMEM((8 * GRID, CAP), jnp.float32),
                pltpu.VMEM((GRID, 2 * GRID), jnp.bfloat16),
            ],
        )(planes, x_high, x_low, y_table)

    me = lax.axis_index("gz").astype(jnp.int32).reshape(1)
    sent = call(
        pack_blocks,
        rows_of(128 * 16),
        [smem()] * 4 + [vmem()] * 2,
        vmem(),
        scratch_shapes=[pltpu.SMEM((n,), jnp.int32) for n in (256, 264, 128, 16)],
    )(me, *points)
    held = swap(sent.reshape(128, 16, CAP), AXES)
    heads = held[:, 15, :SLOTS].astype(jnp.int32).reshape(128 * SLOTS)
    held = held.reshape(128 * 16, CAP)
    strays, rows, tiles, note = call(
        sort_blocks,
        (rows_of(8 * ROWS_S), ints(392), ints(392), ints(2)),
        [smem(), smem(), vmem()],
        (vmem(), smem(), smem(), smem()),
        scratch_shapes=[pltpu.SMEM((392,), jnp.int32), pltpu.SMEM((8,), jnp.int32)],
    )(me, heads, held)
    strays = swap(strays.reshape(8, ROWS_S, CAP), "gz")
    grid = call(
        spread_direct,
        rows_of(16384),
        [smem(), smem(), smem(), vmem()],
        vmem(),
        cost_estimate=pl.CostEstimate(flops=3 * 10**10, bytes_accessed=10**8, transcendentals=0),
    )(note, rows, tiles, held)
    stray_heads = strays[:, 5 * STRAYS].astype(jnp.int32)
    density, mark = finish(note, stray_heads, strays.reshape(8 * ROWS_S, CAP), grid)

    def general(state):
        _, again, *given = lax.optimization_barrier((*state, *points))
        parts = call(
            pack_bricks,
            rows_of(16 * ROWS1),
            [smem()] * 3 + [vmem()] * 2,
            vmem(),
            scratch_shapes=[pltpu.SMEM((16,), jnp.int32)],
        )(*given)
        parts = swap(parts.reshape(16, ROWS1, CAP), "brick")
        head = parts[:, 5 * PER_DEST].astype(jnp.int32)
        parts = parts.reshape(16 * ROWS1, CAP)

        def another(inner):
            turn, _, total = inner
            packed = call(
                pack_tiles,
                rows_of(8 * ROWS2),
                [smem(), smem(), vmem()],
                vmem(),
                scratch_shapes=[pltpu.SMEM((8,), jnp.int32)],
            )(turn, head, parts)
            blocks = swap(packed.reshape(8, ROWS2, CAP), "gz")
            told = blocks[:, 5 * ROOM : 5 * ROOM + 2].astype(jnp.int32)
            total = call(
                spread_round,
                rows_of(16384),
                [smem(), vmem(), anywhere()],
                vmem(),
                scratch_shapes=[
                    pltpu.SMEM((8 * ROOM,), jnp.int32),
                    pltpu.SMEM((8 * ROOM,), jnp.int32),
                    pltpu.SemaphoreType.DMA,
                ],
            )(told[:, 0], blocks.reshape(8 * ROWS2, CAP), total)
            return turn + 1, ((jnp.max(told[:, 1]) + ROOM - 1) // ROOM).reshape(1), total

        _, _, total = lax.while_loop(
            lambda inner: inner[0][0] < inner[1][0],
            another,
            (
                jnp.zeros((1,), jnp.int32),
                jnp.ones((1,), jnp.int32),
                jnp.zeros((16384, CAP), jnp.float32),
            ),
        )
        none = jnp.zeros((8, CAP), jnp.int32)
        return finish(
            jnp.zeros((2,), jnp.int32),
            none,
            jnp.zeros((8 * ROWS_S, CAP), jnp.float32),
            total,
        )

    density, _ = lax.while_loop(lambda state: state[1][0] > 0, general, (density, mark))
    return density


def solution(mesh):
    in_specs = (
        P("gz", "brick", None, None),
        P("gz", "brick", None, None),
        P("gz", "brick", None),
        P("gz", "brick"),
        P("gz", "brick"),
    )
    out_specs = P(None, AXES, None, None)
    inverse = 1.0 / correction_of(GRID)
    z_high, z_low = quarter_tables(inverse * GRID ** (-1.5))
    x_high, x_low = quarter_tables(inverse)
    y_table = full_table(inverse)

    def whole(*args):
        tables = [jnp.asarray(t) for t in (z_high, z_low, x_high, x_low, y_table)]
        return jax.shard_map(
            functools.partial(body),
            mesh=mesh,
            in_specs=(P(),) * 5 + in_specs,
            out_specs=out_specs,
            check_vma=False,
        )(*tables, *args)

    return whole
```

```python
import functools
import math

import jax
import jax.numpy as jnp
import ml_dtypes
import numpy as np
from jax import lax
from jax.experimental import pallas as pl
from jax.experimental.pallas import tpu as pltpu
from jax.sharding import PartitionSpec as P

GRID = 512
TX = 16
TZ = 4
CAP = 128
AXES = ("brick", "gz")
PER_DEST = 24
ROWS1 = 5 * PER_DEST + 8
ROOM = 80
ROWS2 = 5 * ROOM + 8
LAST = 127
SLOTS = 3
STRAYS = 32
ROWS_S = 5 * STRAYS + 8
MARK = 1e30
GROUP = 16
GROUP_LISTED = 32
DEPTH = 24
WIDE = 136
MIB = 1024 * 1024
VMEM_MIB = {
    "pack_blocks": 8,
    "sort_blocks": 8,
    "spread_direct": 54,
    "spread_and_turn": 54,
    "turn_planes": 28,
}


def correction_of(length):
    places = np.arange(length)
    shifted = np.where(places < length // 2, places, places - length)
    nodes = np.arange(-63, 64)
    weights = np.maximum(0.0, 1.0 - (nodes / 32.0) ** 2 / 4.0) ** 10
    phases = shifted[:, None] * nodes[None, :] * (2.0 * math.pi / (32.0 * length))
    return np.sum(weights[None, :] * np.cos(phases), axis=1) / 32.0


def split(table):
    high = table.astype(np.float32).astype(ml_dtypes.bfloat16)
    low = (table - high.astype(np.float64)).astype(np.float32).astype(ml_dtypes.bfloat16)
    return high, low


def quarter_tables(scale):
    k, b = np.arange(128)[:, None], np.arange(128)[None, :]
    out = []
    for r in range(4):
        turned = (b * (4 * k + r)) % GRID
        angle = turned * (2.0 * math.pi / GRID)
        gain = scale[4 * np.arange(128) + r][:, None]
        c, s = np.cos(angle) * gain, np.sin(angle) * gain
        out.append(np.block([[c, -s], [s, c]]))
    return split(np.stack(out))


def full_table(scale):
    y, k = np.arange(GRID)[:, None], np.arange(GRID)[None, :]
    angle = (y * k % GRID) * (2.0 * math.pi / GRID)
    c, s = np.cos(angle) * scale[None, :], np.sin(angle) * scale[None, :]
    return np.block([[c, s], [-s, c]]).astype(np.float32).astype(ml_dtypes.bfloat16)


def lanes():
    return lax.broadcasted_iota(jnp.int32, (1, CAP), 1)


def pack_blocks(
    me_ref, brick_ref, tile_ref, live_ref, spots_ref, values_ref, out_ref,
    place_ref, left_ref, count_ref, turn_ref,
):
    lane = lanes()

    def clear(k, carry):
        count_ref[k] = 0
        out_ref[pl.ds(k * 16 + 15, 1), :] = jnp.full((1, CAP), -1.0, jnp.float32)
        return carry

    lax.fori_loop(0, 128, clear, 0, unroll=8)
    for b in range(16):
        turn_ref[b] = me_ref[0]

    def direct(i, left):
        key = brick_ref[i] * 8 + lax.shift_right_logical(tile_ref[i], 4)
        count = count_ref[key]
        place_ref[i] = key * 16 + count
        count_ref[key] = jnp.minimum(count + 1, SLOTS)
        left_ref[left] = i
        return left + (count >= SLOTS).astype(jnp.int32)

    strays = lax.fori_loop(0, 256, direct, 0, unroll=4)

    def stray(n, carry):
        i = left_ref[n]
        b = brick_ref[i]
        turn = lax.while_loop(
            lambda p: count_ref[b * 8 + (p & 7)] >= SLOTS, lambda p: p + 1, turn_ref[b]
        )
        key = b * 8 + (turn & 7)
        place_ref[i] = key * 16 + count_ref[key]
        count_ref[key] = count_ref[key] + 1
        turn_ref[b] = turn
        return carry

    lax.fori_loop(0, strays, stray, 0)

    def move(i, carry):
        row = place_ref[i]
        slot = row & 15
        for d in range(3):
            out_ref[pl.ds(row + d * SLOTS, 1), :] = spots_ref[d, pl.ds(i, 1), :]
        live = lane < live_ref[i]
        for d in range(2):
            out_ref[pl.ds(row + (3 + d) * SLOTS, 1), :] = jnp.where(
                live, values_ref[i, d : d + 1, :], 0.0
            )
        head = pl.ds(row - slot + 15, 1)
        out_ref[head, :] = jnp.where(lane == slot, tile_ref[i].astype(jnp.float32), out_ref[head, :])
        return carry

    lax.fori_loop(0, 256, move, 0, unroll=8)


def sort_blocks(
    me_ref, head_ref, data_ref, out_ref, row_ref, tile_ref, note_ref, left_ref, count_ref
):
    lane = lanes()
    me = me_ref[0]
    for t in range(8):
        count_ref[t] = 0
        out_ref[t * ROWS_S + 5 * STRAYS : (t + 1) * ROWS_S, :] = jnp.zeros((8, CAP), jnp.float32)

    def look(n, found):
        own, strays = found
        source = (n & 15) * 8 + lax.shift_right_logical(n, 4)
        for c in range(SLOTS):
            tile = head_ref[source * SLOTS + c]
            tx = lax.shift_right_arithmetic(tile, 4)
            straight = (tx == me).astype(jnp.int32)
            row_ref[own] = source * 16 + c
            tile_ref[own] = (source & 7) * 16 + (tile & 15)
            own = own + straight
            left_ref[strays] = source * SLOTS + c
            strays = strays + (tile >= 0).astype(jnp.int32) - straight
        note_ref[2 + lax.shift_right_logical(n, 4)] = own
        return own, strays

    own, strays = lax.fori_loop(0, 128, look, (0, 0), unroll=2)

    def forward(n, carry):
        entry = left_ref[n]
        source = entry // SLOTS
        row = source * 16 + entry - source * SLOTS
        tile = head_ref[entry]
        tx = lax.shift_right_logical(tile, 4)
        k = count_ref[tx]
        count_ref[tx] = k + 1
        k = jnp.minimum(k, STRAYS - 1)
        for d in range(5):
            out_ref[pl.ds(tx * ROWS_S + d * STRAYS + k, 1), :] = data_ref[
                pl.ds(row + d * SLOTS, 1), :
            ]
        head = pl.ds(tx * ROWS_S + 5 * STRAYS, 1)
        depth = ((source & 7) * 16 + (tile & 15)).astype(jnp.float32)
        out_ref[head, :] = jnp.where(lane == k, depth, out_ref[head, :])
        return carry

    lax.fori_loop(0, strays, forward, 0)
    most = count_ref[0]
    for t in range(8):
        row = t * ROWS_S + 5 * STRAYS
        count = count_ref[t]
        most = jnp.maximum(most, count)
        sent = jnp.minimum(count, STRAYS).astype(jnp.float32)
        out_ref[row : row + 1, :] = jnp.where(lane == LAST, sent, out_ref[row : row + 1, :])
    note_ref[0] = own
    note_ref[1] = (most > STRAYS).astype(jnp.int32)


def pack_bricks(brick_ref, tile_ref, live_ref, spots_ref, values_ref, out_ref, count_ref):
    lane = lanes()
    for b in range(16):
        count_ref[b] = 0
        out_ref[b * ROWS1 + 5 * PER_DEST : (b + 1) * ROWS1, :] = jnp.zeros((8, CAP), jnp.float32)

    def step(i, tally):
        b = brick_ref[i]
        r = count_ref[b]
        count_ref[b] = r + 1
        base = b * ROWS1
        for d in range(3):
            out_ref[pl.ds(base + d * PER_DEST + r, 1), :] = spots_ref[d, pl.ds(i, 1), :]
        live = lane < live_ref[i]
        for d in range(2):
            out_ref[pl.ds(base + (3 + d) * PER_DEST + r, 1), :] = jnp.where(
                live, values_ref[i, d : d + 1, :], 0.0
            )
        head = pl.ds(base + 5 * PER_DEST, 1)
        tile = tile_ref[i]
        out_ref[head, :] = jnp.where(lane == r, tile.astype(jnp.float32), out_ref[head, :])
        key = b * 8 + lax.shift_right_logical(tile, 4)
        return tally + jnp.where(lane == key, 1.0, 0.0)

    tally = lax.fori_loop(0, 256, step, jnp.zeros((1, CAP), jnp.float32), unroll=4)
    for b in range(16):
        row = b * ROWS1 + 5 * PER_DEST
        total = count_ref[b].astype(jnp.float32)
        out_ref[row : row + 1, :] = jnp.where(lane == LAST, total, out_ref[row : row + 1, :])
        out_ref[row + 1 : row + 2, :] = tally


def pack_tiles(round_ref, head_ref, data_ref, out_ref, count_ref):
    lane = lanes()
    first = round_ref[0] * ROOM
    for t in range(8):
        count_ref[t] = 0
        out_ref[t * ROWS2 + 5 * ROOM : (t + 1) * ROWS2, :] = jnp.zeros((8, CAP), jnp.float32)
    spare = 5 * ROOM + 7

    def source(s, carry):
        held = head_ref[s, LAST]

        def step(i, inner):
            tile = head_ref[s, i]
            live = i < held
            tx = lax.shift_right_logical(tile, 4)
            place = count_ref[tx]
            count_ref[tx] = place + live.astype(jnp.int32)
            k = place - first
            good = live & (k >= 0) & (k < ROOM)
            base = tx * ROWS2
            for d in range(5):
                row = jnp.where(good, base + d * ROOM + k, spare)
                out_ref[pl.ds(row, 1), :] = data_ref[pl.ds(s * ROWS1 + d * PER_DEST + i, 1), :]
            head = pl.ds(base + 5 * ROOM, 1)
            depth = (tile & 15).astype(jnp.float32)
            spot = jnp.where(good, k, -1)
            out_ref[head, :] = jnp.where(lane == spot, depth, out_ref[head, :])
            return inner

        return lax.fori_loop(0, PER_DEST, step, carry, unroll=4)

    lax.fori_loop(0, 16, source, 0)
    tally = data_ref[5 * PER_DEST + 1 : 5 * PER_DEST + 2, :]
    for s in range(1, 16):
        row = s * ROWS1 + 5 * PER_DEST + 1
        tally = tally + data_ref[row : row + 1, :]
    for t in range(8):
        row = t * ROWS2 + 5 * ROOM
        count = count_ref[t]
        sent = jnp.clip(count - first, 0, ROOM).astype(jnp.float32)
        out_ref[row : row + 1, :] = jnp.where(lane == LAST, sent, out_ref[row : row + 1, :])
        out_ref[row + 1 : row + 2, :] = tally


def phi10(t):
    square = t * t
    fourth = square * square
    return fourth * fourth * square


def weights_at(cells, position):
    half = cells - 0.5 * position
    return phi10(jnp.maximum(0.0, 1.0 - half * half))


def halves(value):
    high = value.astype(jnp.bfloat16)
    return high, (value - high.astype(jnp.float32)).astype(jnp.bfloat16)


def block_cells(data_ref, row, step, scale):
    def at(d):
        return data_ref[pl.ds(row + d * step, 1), :]

    pos_x = -1.0 + (TX + 2) * at(0)
    pos_y = -1.0 + (CAP + 2) * at(1)
    pos_z = -1.0 + (TZ + 2) * at(2)
    half_cells = 0.5 * lax.broadcasted_iota(jnp.int32, (TX, CAP), 0).astype(jnp.float32)
    wx = weights_at(half_cells, pos_x).astype(jnp.bfloat16).astype(jnp.float32)
    wz = weights_at(half_cells[:8], pos_z)
    parts = []
    for d in (3, 4):
        wzv = wz * (at(d) * scale)
        for l in range(TZ):
            parts.append(wx * wzv[l : l + 1, :])
    left_high, left_low = halves(jnp.concatenate(parts, axis=0))
    first = jnp.floor(pos_y) - 1.0
    near_high, near_low = halves(weights_at(half_cells[:8], pos_y - first))
    cells = lax.broadcasted_iota(jnp.int32, (CAP, CAP), 0).astype(jnp.float32)
    place = cells.astype(jnp.bfloat16) - first.astype(jnp.bfloat16)
    high = jnp.zeros((CAP, CAP), jnp.bfloat16)
    low = high
    for k in range(4):
        here = place == jnp.bfloat16(k)
        high = jnp.where(here, near_high[k : k + 1, :], high)
        low = jnp.where(here, near_low[k : k + 1, :], low)
    return lax.dot_general(
        jnp.concatenate([left_high, left_high, left_low], axis=1),
        jnp.concatenate([high, low, high], axis=1),
        (((1,), (1,)), ((), ())),
        preferred_element_type=jnp.float32,
    )


def add_listed(row_ref, tile_ref, held, step, data_ref, grid_ref, depth, size, after=None):
    def group(n, carry):
        found = []
        for u in range(size):
            i = n * size + u
            live = i < held
            i = jnp.where(live, i, 0)
            scale = jnp.where(live, 1.0, 0.0).astype(jnp.float32)
            found.append((tile_ref[i], block_cells(data_ref, row_ref[i], step, scale)))
        for tile, cells in found:
            for a in range(2):
                for l in range(TZ):
                    start = (a * 512 + tile * TZ + l) * depth
                    rows = pl.ds(pl.multiple_of(start, 8), TX)
                    part = (a * TZ + l) * TX
                    grid_ref[rows, :] += cells[part : part + TX]
        return carry if after is None else after((n + 1) * size, carry)

    return lax.fori_loop(0, (held + size - 1) // size, group, 0)


def list_headed(head_ref, row_ref, tile_ref, room, base):
    def source(g, total):
        def entry(i, at):
            row_ref[at] = g * (5 * room + 8) + i
            tile_ref[at] = head_ref[g, i] + base * g
            return at + 1

        return lax.fori_loop(0, head_ref[g, LAST], entry, total)

    return lax.fori_loop(0, 8, source, 0)


def clear_grid(grid_ref):
    def clear(i, carry):
        grid_ref[pl.ds(pl.multiple_of(i * 64, 64), 64), :] = jnp.zeros((64, CAP), jnp.float32)
        return carry

    lax.fori_loop(0, 16384 // 64, clear, 0, unroll=4)


def spread_direct(note_ref, row_ref, tile_ref, data_ref, out_ref, grid_ref, sem):
    clear_grid(grid_ref)

    def outward(a, slab):
        rows = pl.ds(pl.multiple_of(a * 8192 + slab * 1024, 1024), 1024)
        return pltpu.make_async_copy(grid_ref.at[rows], out_ref.at[rows], sem.at[a, slab])

    def leave(slab):
        for a in range(2):
            outward(a, slab).start()
        return slab + 1

    def after(done, slab):
        return lax.while_loop(
            lambda at: (at < 8) & (note_ref[2 + jnp.minimum(at, 7)] <= done), leave, slab
        )

    held = note_ref[0]
    slab = add_listed(
        row_ref, tile_ref, held, SLOTS, data_ref, grid_ref, TX, GROUP_LISTED, after
    )
    lax.while_loop(lambda at: at < 8, leave, slab)
    for slab in range(8):
        for a in range(2):
            outward(a, slab).wait()


def spread_round(head_ref, data_ref, from_ref, grid_ref, row_ref, tile_ref, sem):
    copy = pltpu.make_async_copy(from_ref, grid_ref, sem)
    copy.start()
    copy.wait()
    held = list_headed(head_ref, row_ref, tile_ref, ROOM, 16)
    add_listed(row_ref, tile_ref, held, ROOM, data_ref, grid_ref, TX, GROUP)


def quarters(re, im):
    s02r, s02i = re[0] + re[2], im[0] + im[2]
    d02r, d02i = re[0] - re[2], im[0] - im[2]
    s13r, s13i = re[1] + re[3], im[1] + im[3]
    d13r, d13i = re[1] - re[3], im[1] - im[3]
    return [
        (s02r + s13r, s02i + s13i),
        (d02r - d13i, d02i + d13r),
        (s02r - s13r, s02i - s13i),
        (d02r + d13i, d02i - d13r),
    ]


def three_pass(high, low, value):
    top, rest = halves(value)

    def dot(a, b):
        return jnp.dot(a, b, preferred_element_type=jnp.float32)

    return dot(high, top) + (dot(high, rest) + dot(low, top))


def spread_and_turn(
    note_ref, head_ref, data_ref, high_ref, low_ref, from_ref, out_ref,
    grid_ref, sent_ref, row_ref, tile_ref, sem, out_sem,
):
    copy = pltpu.make_async_copy(from_ref, grid_ref.at[:, pl.ds(0, TX), :], sem)
    copy.start()
    held = list_headed(head_ref, row_ref, tile_ref, STRAYS, 0)
    copy.wait()
    flat = grid_ref.reshape(1024 * DEPTH, CAP)
    sent = sent_ref.reshape(128 * WIDE, CAP)
    add_listed(row_ref, tile_ref, held, STRAYS, data_ref, flat, DEPTH, GROUP)

    def columns(n, carry):
        j = 2 * n

        def plane(a, q):
            return jnp.concatenate(
                [
                    flat[pl.ds((a * 512 + q * 128) * DEPTH + j + u, 128, stride=DEPTH), :]
                    for u in range(2)
                ],
                axis=1,
            )

        re = [plane(0, q) for q in range(4)]
        im = [plane(1, q) for q in range(4)]
        for r, (real, imag) in enumerate(quarters(re, im)):
            turned = three_pass(high_ref[r], low_ref[r], jnp.concatenate([real, imag], axis=0))
            for a in range(2):
                for u in range(2):
                    sent[pl.ds(r * 32 + a * 16 + j + u, 128, stride=WIDE), :] = turned[
                        a * 128 : (a + 1) * 128, u * 128 : (u + 1) * 128
                    ]
        return carry

    def outward(n):
        return pltpu.make_async_copy(sent_ref.at[:, n], out_ref.at[:, n], out_sem.at[n])

    lax.fori_loop(0, 4, columns, 0)

    @pl.when(note_ref[1] > 0)
    def _():
        sent[pl.ds(0, 128, stride=WIDE), :] = jnp.full((128, CAP), MARK, jnp.float32)

    for n in range(8):
        outward(2 * n).start()
    lax.fori_loop(4, 8, columns, 0)
    for n in range(8):
        outward(2 * n + 1).start()
    for n in range(16):
        outward(n).wait()


def turn_planes(data_ref, high_ref, low_ref, y_ref, out_ref, mark_ref, rows_ref, left_ref):
    @pl.when(pl.program_id(0) == 0)
    def _():
        most = data_ref[0, 0, :, 0, 0, 0]
        for n in range(1, 16):
            most = jnp.maximum(most, data_ref[n // 4, n % 4, :, 0, 0, 0])
        mark_ref[0] = (jnp.max(most) > 0.1 * MARK).astype(jnp.int32)

    def plane(c, bx, by):
        return data_ref[bx, by, :, 0, c].reshape(128, CAP)

    for pair in range(2):
        ys = (2 * pair, 2 * pair + 1)
        re = [jnp.concatenate([plane(0, bx, by) for by in ys], axis=1) for bx in range(4)]
        im = [jnp.concatenate([plane(1, bx, by) for by in ys], axis=1) for bx in range(4)]
        for r, (real, imag) in enumerate(quarters(re, im)):
            turned = three_pass(high_ref[r], low_ref[r], jnp.concatenate([real, imag], axis=0))
            for a in range(2):
                for u in range(2):
                    start = (a * 4 + ys[u]) * GRID + r
                    rows_ref[pl.ds(start, 128, stride=4), :] = turned[
                        a * 128 : (a + 1) * 128, u * 128 : (u + 1) * 128
                    ]
    for n in range(8):
        left_ref[:, n * 128 : (n + 1) * 128] = rows_ref[n * GRID : (n + 1) * GRID, :].astype(
            jnp.bfloat16
        )
    for n in range(4):
        out_ref[n // 2, 0, :, (n % 2) * 256 : (n % 2 + 1) * 256] = jnp.dot(
            left_ref[...], y_ref[:, n * 256 : (n + 1) * 256], preferred_element_type=jnp.float32
        )


def smem():
    return pl.BlockSpec(memory_space=pltpu.SMEM)


def vmem():
    return pl.BlockSpec(memory_space=pltpu.VMEM)


def params(name):
    return pltpu.CompilerParams(vmem_limit_bytes=VMEM_MIB.get(name, 40) * MIB)


def swap(array, axis):
    return lax.all_to_all(array, axis, split_axis=0, concat_axis=0, tiled=True)


def call(kernel, out_shape, in_specs, out_specs, **options):
    return pl.pallas_call(
        kernel,
        out_shape=out_shape,
        in_specs=in_specs,
        out_specs=out_specs,
        compiler_params=params(kernel.__name__),
        name=kernel.__name__,
        **options,
    )


def anywhere():
    return pl.BlockSpec(memory_space=pl.ANY)


def large():
    return pl.BlockSpec(memory_space=pl.ANY)


def rows_of(rows):
    return jax.ShapeDtypeStruct((rows, CAP), jnp.float32)


def ints(count):
    return jax.ShapeDtypeStruct((count,), jnp.int32)


def body(z_high, z_low, x_high, x_low, y_table, spots, values, dest_brick, dest_tile, live_count):
    points = (
        dest_brick.reshape(256),
        dest_tile[0],
        live_count[0],
        spots[0].transpose(1, 0, 2),
        values[0],
    )

    def finish(note, heads, data, grid):
        columns = call(
            spread_and_turn,
            jax.ShapeDtypeStruct((128, 16, 8, CAP), jnp.float32),
            [smem(), smem(), vmem(), vmem(), vmem(), anywhere()],
            large(),
            scratch_shapes=[
                pltpu.VMEM((1024, DEPTH, CAP), jnp.float32),
                pltpu.VMEM((128, WIDE // 8, 8, CAP), jnp.float32),
                pltpu.SMEM((8 * STRAYS,), jnp.int32),
                pltpu.SMEM((8 * STRAYS,), jnp.int32),
                pltpu.SemaphoreType.DMA,
                pltpu.SemaphoreType.DMA((16,)),
            ],
        )(note, heads, data, z_high, z_low, grid.reshape(1024, TX, CAP))
        planes = swap(columns.reshape(128, 4, 2, TX, CAP), AXES).reshape(4, 4, 8, 4, 2, TX, CAP)
        return call(
            turn_planes,
            (jax.ShapeDtypeStruct((2, 4, GRID, GRID), jnp.float32), ints(1)),
            [
                pl.BlockSpec((4, 4, 8, 1, 2, TX, CAP), lambda q: (0, 0, 0, q, 0, 0, 0)),
                vmem(),
                vmem(),
                vmem(),
            ],
            (pl.BlockSpec((2, 1, GRID, GRID), lambda q: (0, q, 0, 0)), smem()),
            grid=(4,),
            scratch_shapes=[
                pltpu.VMEM((8 * GRID, CAP), jnp.float32),
                pltpu.VMEM((GRID, 2 * GRID), jnp.bfloat16),
            ],
        )(planes, x_high, x_low, y_table)

    me = lax.axis_index("gz").astype(jnp.int32).reshape(1)
    sent = call(
        pack_blocks,
        rows_of(128 * 16),
        [smem()] * 4 + [vmem()] * 2,
        vmem(),
        scratch_shapes=[pltpu.SMEM((n,), jnp.int32) for n in (256, 264, 128, 16)],
    )(me, *points)
    held = swap(sent.reshape(128, 16, CAP), AXES)
    heads = held[:, 15, :SLOTS].astype(jnp.int32).reshape(128 * SLOTS)
    held = held.reshape(128 * 16, CAP)
    strays, rows, tiles, note = call(
        sort_blocks,
        (rows_of(8 * ROWS_S), ints(392), ints(392), ints(16)),
        [smem(), smem(), vmem()],
        (vmem(), smem(), smem(), smem()),
        scratch_shapes=[pltpu.SMEM((392,), jnp.int32), pltpu.SMEM((8,), jnp.int32)],
    )(me, heads, held)
    strays = swap(strays.reshape(8, ROWS_S, CAP), "gz")
    grid = call(
        spread_direct,
        rows_of(16384),
        [smem(), smem(), smem(), vmem()],
        large(),
        scratch_shapes=[pltpu.VMEM((16384, CAP), jnp.float32), pltpu.SemaphoreType.DMA((2, 8))],
        cost_estimate=pl.CostEstimate(flops=3 * 10**10, bytes_accessed=10**8, transcendentals=0),
    )(note, rows, tiles, held)
    stray_heads = strays[:, 5 * STRAYS].astype(jnp.int32)
    density, mark = finish(note, stray_heads, strays.reshape(8 * ROWS_S, CAP), grid)

    def general(state):
        _, again, *given = lax.optimization_barrier((*state, *points))
        parts = call(
            pack_bricks,
            rows_of(16 * ROWS1),
            [smem()] * 3 + [vmem()] * 2,
            vmem(),
            scratch_shapes=[pltpu.SMEM((16,), jnp.int32)],
        )(*given)
        parts = swap(parts.reshape(16, ROWS1, CAP), "brick")
        head = parts[:, 5 * PER_DEST].astype(jnp.int32)
        parts = parts.reshape(16 * ROWS1, CAP)

        def another(inner):
            turn, _, total = inner
            packed = call(
                pack_tiles,
                rows_of(8 * ROWS2),
                [smem(), smem(), vmem()],
                vmem(),
                scratch_shapes=[pltpu.SMEM((8,), jnp.int32)],
            )(turn, head, parts)
            blocks = swap(packed.reshape(8, ROWS2, CAP), "gz")
            told = blocks[:, 5 * ROOM : 5 * ROOM + 2].astype(jnp.int32)
            total = call(
                spread_round,
                rows_of(16384),
                [smem(), vmem(), anywhere()],
                vmem(),
                scratch_shapes=[
                    pltpu.SMEM((8 * ROOM,), jnp.int32),
                    pltpu.SMEM((8 * ROOM,), jnp.int32),
                    pltpu.SemaphoreType.DMA,
                ],
            )(told[:, 0], blocks.reshape(8 * ROWS2, CAP), total)
            return turn + 1, ((jnp.max(told[:, 1]) + ROOM - 1) // ROOM).reshape(1), total

        _, _, total = lax.while_loop(
            lambda inner: inner[0][0] < inner[1][0],
            another,
            (
                jnp.zeros((1,), jnp.int32),
                jnp.ones((1,), jnp.int32),
                jnp.zeros((16384, CAP), jnp.float32),
            ),
        )
        none = jnp.zeros((8, CAP), jnp.int32)
        return finish(
            jnp.zeros((16,), jnp.int32),
            none,
            jnp.zeros((8 * ROWS_S, CAP), jnp.float32),
            total,
        )

    density, _ = lax.while_loop(lambda state: state[1][0] > 0, general, (density, mark))
    return density


def solution(mesh):
    in_specs = (
        P("gz", "brick", None, None),
        P("gz", "brick", None, None),
        P("gz", "brick", None),
        P("gz", "brick"),
        P("gz", "brick"),
    )
    out_specs = P(None, AXES, None, None)
    inverse = 1.0 / correction_of(GRID)
    z_high, z_low = quarter_tables(inverse * GRID ** (-1.5))
    x_high, x_low = quarter_tables(inverse)
    y_table = full_table(inverse)

    def whole(*args):
        tables = [jnp.asarray(t) for t in (z_high, z_low, x_high, x_low, y_table)]
        return jax.shard_map(
            functools.partial(body),
            mesh=mesh,
            in_specs=(P(),) * 5 + in_specs,
            out_specs=out_specs,
            check_vma=False,
        )(*tables, *args)

    return whole
```

```python
import functools
import math

import jax
import jax.numpy as jnp
import ml_dtypes
import numpy as np
from jax import lax
from jax.experimental import pallas as pl
from jax.experimental.pallas import tpu as pltpu
from jax.sharding import PartitionSpec as P

GRID = 512
TX = 16
TZ = 4
CAP = 128
AXES = ("brick", "gz")
PER_DEST = 24
ROWS1 = 5 * PER_DEST + 8
ROOM = 80
ROWS2 = 5 * ROOM + 8
LAST = 127
SLOTS = 3
STRAYS = 32
ROWS_S = 5 * STRAYS + 8
MARK = 1e30
GROUP = 16
GROUP_LISTED = 32
LISTED = 16
STRAYED = LISTED + 392
LIST = STRAYED + 392
DEPTH = 24
WIDE = 136
MIB = 1024 * 1024
VMEM_MIB = {
    "pack_blocks": 8,
    "sort_blocks": 8,
    "spread_direct": 54,
    "spread_and_turn": 54,
    "turn_planes": 28,
}


def correction_of(length):
    places = np.arange(length)
    shifted = np.where(places < length // 2, places, places - length)
    nodes = np.arange(-63, 64)
    weights = np.maximum(0.0, 1.0 - (nodes / 32.0) ** 2 / 4.0) ** 10
    phases = shifted[:, None] * nodes[None, :] * (2.0 * math.pi / (32.0 * length))
    return np.sum(weights[None, :] * np.cos(phases), axis=1) / 32.0


def split(table):
    high = table.astype(np.float32).astype(ml_dtypes.bfloat16)
    low = (table - high.astype(np.float64)).astype(np.float32).astype(ml_dtypes.bfloat16)
    return high, low


def quarter_tables(scale):
    k, b = np.arange(128)[:, None], np.arange(128)[None, :]
    out = []
    for r in range(4):
        turned = (b * (4 * k + r)) % GRID
        angle = turned * (2.0 * math.pi / GRID)
        gain = scale[4 * np.arange(128) + r][:, None]
        c, s = np.cos(angle) * gain, np.sin(angle) * gain
        out.append(np.block([[c, -s], [s, c]]))
    return split(np.stack(out))


def full_table(scale):
    y, k = np.arange(GRID)[:, None], np.arange(GRID)[None, :]
    angle = (y * k % GRID) * (2.0 * math.pi / GRID)
    c, s = np.cos(angle) * scale[None, :], np.sin(angle) * scale[None, :]
    return np.block([[c, s], [-s, c]]).astype(np.float32).astype(ml_dtypes.bfloat16)


def lanes():
    return lax.broadcasted_iota(jnp.int32, (1, CAP), 1)


def pack_blocks(
    me_ref, brick_ref, tile_ref, live_ref, spots_ref, values_ref, out_ref,
    place_ref, left_ref, count_ref, turn_ref,
):
    lane = lanes()

    def clear(k, carry):
        count_ref[k] = 0
        out_ref[pl.ds(k * 16 + 15, 1), :] = jnp.full((1, CAP), -1.0, jnp.float32)
        return carry

    lax.fori_loop(0, 128, clear, 0, unroll=8)
    for b in range(16):
        turn_ref[b] = me_ref[0]

    def place(i, left):
        key = brick_ref[i] * 8 + lax.shift_right_logical(tile_ref[i], 4)
        count = count_ref[key]
        place_ref[i] = key * 16 + count
        count_ref[key] = jnp.minimum(count + 1, SLOTS)
        left_ref[left] = i
        return left + (count >= SLOTS).astype(jnp.int32)

    strays = lax.fori_loop(0, 256, place, 0, unroll=16)

    def stray(n, carry):
        i = left_ref[n]
        b = brick_ref[i]
        turn = lax.while_loop(
            lambda p: count_ref[b * 8 + (p & 7)] >= SLOTS, lambda p: p + 1, turn_ref[b]
        )
        key = b * 8 + (turn & 7)
        place_ref[i] = key * 16 + count_ref[key]
        count_ref[key] = count_ref[key] + 1
        turn_ref[b] = turn
        return carry

    lax.fori_loop(0, strays, stray, 0)

    def move(i, carry):
        row = place_ref[i]
        slot = row & 15
        for d in range(3):
            out_ref[pl.ds(row + d * SLOTS, 1), :] = spots_ref[d, pl.ds(i, 1), :]
        live = lane < live_ref[i]
        for d in range(2):
            out_ref[pl.ds(row + (3 + d) * SLOTS, 1), :] = jnp.where(
                live, values_ref[i, d : d + 1, :], 0.0
            )
        head = pl.ds(row - slot + 15, 1)
        out_ref[head, :] = jnp.where(lane == slot, tile_ref[i].astype(jnp.float32), out_ref[head, :])
        return carry

    lax.fori_loop(0, 256, move, 0, unroll=8)


def sort_blocks(me_ref, head_ref, data_ref, out_ref, list_ref, count_ref):
    lane = lanes()
    me = me_ref[0]
    for t in range(8):
        count_ref[t] = 0
        out_ref[t * ROWS_S + 5 * STRAYS : (t + 1) * ROWS_S, :] = jnp.zeros((8, CAP), jnp.float32)

    def look(n, found):
        own, strays = found
        source = (n & 15) * 8 + lax.shift_right_logical(n, 4)
        for c in range(SLOTS):
            tile = head_ref[source * SLOTS + c]
            straight = lax.shift_right_arithmetic(tile, 4) == me
            at = jnp.where(straight, LISTED + own, STRAYED + strays)
            list_ref[at] = (source * 16 + c) * 128 + tile
            own = own + straight.astype(jnp.int32)
            strays = strays + ((tile >= 0) & ~straight).astype(jnp.int32)
        list_ref[2 + lax.shift_right_logical(n, 4)] = own
        return own, strays

    own, strays = lax.fori_loop(0, 128, look, (0, 0), unroll=4)

    def forward(n, carry):
        code = list_ref[STRAYED + n]
        row = lax.shift_right_logical(code, 7)
        tile = code & 127
        tx = lax.shift_right_logical(tile, 4)
        k = count_ref[tx]
        count_ref[tx] = k + 1
        k = jnp.minimum(k, STRAYS - 1)
        for d in range(5):
            out_ref[pl.ds(tx * ROWS_S + d * STRAYS + k, 1), :] = data_ref[
                pl.ds(row + d * SLOTS, 1), :
            ]
        head = pl.ds(tx * ROWS_S + 5 * STRAYS, 1)
        depth = (row & 112) + (tile & 15)
        out_ref[head, :] = jnp.where(lane == k, depth.astype(jnp.float32), out_ref[head, :])
        return carry

    lax.fori_loop(0, strays, forward, 0)
    most = count_ref[0]
    for t in range(8):
        row = t * ROWS_S + 5 * STRAYS
        count = count_ref[t]
        most = jnp.maximum(most, count)
        sent = jnp.minimum(count, STRAYS).astype(jnp.float32)
        out_ref[row : row + 1, :] = jnp.where(lane == LAST, sent, out_ref[row : row + 1, :])
    list_ref[0] = own
    list_ref[1] = (most > STRAYS).astype(jnp.int32)


def pack_bricks(brick_ref, tile_ref, live_ref, spots_ref, values_ref, out_ref, count_ref):
    lane = lanes()
    for b in range(16):
        count_ref[b] = 0
        out_ref[b * ROWS1 + 5 * PER_DEST : (b + 1) * ROWS1, :] = jnp.zeros((8, CAP), jnp.float32)

    def step(i, tally):
        b = brick_ref[i]
        r = count_ref[b]
        count_ref[b] = r + 1
        base = b * ROWS1
        for d in range(3):
            out_ref[pl.ds(base + d * PER_DEST + r, 1), :] = spots_ref[d, pl.ds(i, 1), :]
        live = lane < live_ref[i]
        for d in range(2):
            out_ref[pl.ds(base + (3 + d) * PER_DEST + r, 1), :] = jnp.where(
                live, values_ref[i, d : d + 1, :], 0.0
            )
        head = pl.ds(base + 5 * PER_DEST, 1)
        tile = tile_ref[i]
        out_ref[head, :] = jnp.where(lane == r, tile.astype(jnp.float32), out_ref[head, :])
        key = b * 8 + lax.shift_right_logical(tile, 4)
        return tally + jnp.where(lane == key, 1.0, 0.0)

    tally = lax.fori_loop(0, 256, step, jnp.zeros((1, CAP), jnp.float32), unroll=4)
    for b in range(16):
        row = b * ROWS1 + 5 * PER_DEST
        total = count_ref[b].astype(jnp.float32)
        out_ref[row : row + 1, :] = jnp.where(lane == LAST, total, out_ref[row : row + 1, :])
        out_ref[row + 1 : row + 2, :] = tally


def pack_tiles(round_ref, head_ref, data_ref, out_ref, count_ref):
    lane = lanes()
    first = round_ref[0] * ROOM
    for t in range(8):
        count_ref[t] = 0
        out_ref[t * ROWS2 + 5 * ROOM : (t + 1) * ROWS2, :] = jnp.zeros((8, CAP), jnp.float32)
    spare = 5 * ROOM + 7

    def source(s, carry):
        held = head_ref[s, LAST]

        def step(i, inner):
            tile = head_ref[s, i]
            live = i < held
            tx = lax.shift_right_logical(tile, 4)
            place = count_ref[tx]
            count_ref[tx] = place + live.astype(jnp.int32)
            k = place - first
            good = live & (k >= 0) & (k < ROOM)
            base = tx * ROWS2
            for d in range(5):
                row = jnp.where(good, base + d * ROOM + k, spare)
                out_ref[pl.ds(row, 1), :] = data_ref[pl.ds(s * ROWS1 + d * PER_DEST + i, 1), :]
            head = pl.ds(base + 5 * ROOM, 1)
            depth = (tile & 15).astype(jnp.float32)
            spot = jnp.where(good, k, -1)
            out_ref[head, :] = jnp.where(lane == spot, depth, out_ref[head, :])
            return inner

        return lax.fori_loop(0, PER_DEST, step, carry, unroll=4)

    lax.fori_loop(0, 16, source, 0)
    tally = data_ref[5 * PER_DEST + 1 : 5 * PER_DEST + 2, :]
    for s in range(1, 16):
        row = s * ROWS1 + 5 * PER_DEST + 1
        tally = tally + data_ref[row : row + 1, :]
    for t in range(8):
        row = t * ROWS2 + 5 * ROOM
        count = count_ref[t]
        sent = jnp.clip(count - first, 0, ROOM).astype(jnp.float32)
        out_ref[row : row + 1, :] = jnp.where(lane == LAST, sent, out_ref[row : row + 1, :])
        out_ref[row + 1 : row + 2, :] = tally


def phi10(t):
    square = t * t
    fourth = square * square
    return fourth * fourth * square


def weights_at(cells, position):
    half = cells - 0.5 * position
    return phi10(jnp.maximum(0.0, 1.0 - half * half))


def halves(value):
    high = value.astype(jnp.bfloat16)
    return high, (value - high.astype(jnp.float32)).astype(jnp.bfloat16)


def block_cells(data_ref, row, step, scale):
    def at(d):
        return data_ref[pl.ds(row + d * step, 1), :]

    pos_x = -1.0 + (TX + 2) * at(0)
    pos_y = -1.0 + (CAP + 2) * at(1)
    pos_z = -1.0 + (TZ + 2) * at(2)
    half_cells = 0.5 * lax.broadcasted_iota(jnp.int32, (TX, CAP), 0).astype(jnp.float32)
    wx = weights_at(half_cells, pos_x).astype(jnp.bfloat16).astype(jnp.float32)
    wz = weights_at(half_cells[:8], pos_z)
    parts = []
    for d in (3, 4):
        wzv = wz * (at(d) * scale)
        for l in range(TZ):
            parts.append(wx * wzv[l : l + 1, :])
    left_high, left_low = halves(jnp.concatenate(parts, axis=0))
    first = jnp.floor(pos_y) - 1.0
    near_high, near_low = halves(weights_at(half_cells[:8], pos_y - first))
    cells = lax.broadcasted_iota(jnp.int32, (CAP, CAP), 0).astype(jnp.float32)
    place = cells.astype(jnp.bfloat16) - first.astype(jnp.bfloat16)
    high = jnp.zeros((CAP, CAP), jnp.bfloat16)
    low = high
    for k in range(4):
        here = place == jnp.bfloat16(k)
        high = jnp.where(here, near_high[k : k + 1, :], high)
        low = jnp.where(here, near_low[k : k + 1, :], low)
    return lax.dot_general(
        jnp.concatenate([left_high, left_high, left_low], axis=1),
        jnp.concatenate([high, low, high], axis=1),
        (((1,), (1,)), ((), ())),
        preferred_element_type=jnp.float32,
    )


def add_listed(find, held, step, data_ref, grid_ref, depth, size, before=None, after=None):
    def group(n, carry):
        if before is not None:
            carry = before(jnp.minimum((n + 1) * size, held), carry)
        found = []
        for u in range(size):
            i = n * size + u
            live = i < held
            row, tile = find(jnp.where(live, i, 0))
            scale = jnp.where(live, 1.0, 0.0).astype(jnp.float32)
            found.append((tile, block_cells(data_ref, row, step, scale)))
        for tile, cells in found:
            for a in range(2):
                for l in range(TZ):
                    start = (a * 512 + tile * TZ + l) * depth
                    rows = pl.ds(pl.multiple_of(start, 8), TX)
                    part = (a * TZ + l) * TX
                    grid_ref[rows, :] += cells[part : part + TX]
        return carry if after is None else after((n + 1) * size, carry)

    return lax.fori_loop(0, (held + size - 1) // size, group, 0)


def direct(list_ref):
    def find(i):
        code = list_ref[LISTED + i]
        row = lax.shift_right_logical(code, 7)
        return row, (row & 112) + (code & 15)

    return find


def listed(row_ref, tile_ref):
    return lambda i: (row_ref[i], tile_ref[i])


def list_headed(head_ref, row_ref, tile_ref, room, base):
    def source(g, total):
        def entry(i, at):
            row_ref[at] = g * (5 * room + 8) + i
            tile_ref[at] = head_ref[g, i] + base * g
            return at + 1

        return lax.fori_loop(0, head_ref[g, LAST], entry, total)

    return lax.fori_loop(0, 8, source, 0)


def clear_grid(grid_ref):
    def clear(i, carry):
        grid_ref[pl.ds(pl.multiple_of(i * 64, 64), 64), :] = jnp.zeros((64, CAP), jnp.float32)
        return carry

    lax.fori_loop(0, 16384 // 64, clear, 0, unroll=4)


def list_strays(head_ref, row_ref, tile_ref, ends_ref, next_ref):
    for h in range(8):
        next_ref[h] = 0

    def slab(g, total):
        def source(h, so_far):
            held = head_ref[h, LAST]

            def more(state):
                i, _ = state
                return (i < held) & (lax.shift_right_logical(head_ref[h, i & 63], 4) == g)

            def entry(state):
                i, at = state
                row_ref[at] = h * ROWS_S + i
                tile_ref[at] = head_ref[h, i]
                return i + 1, at + 1

            i, so_far = lax.while_loop(more, entry, (next_ref[h], so_far))
            next_ref[h] = i
            return so_far

        total = lax.fori_loop(0, 8, source, total)
        ends_ref[g] = total
        return total

    return lax.fori_loop(0, 8, slab, 0)


def spread_direct(list_ref, data_ref, out_ref, grid_ref, sem):
    clear_grid(grid_ref)

    def outward(a, slab):
        rows = pl.ds(pl.multiple_of(a * 8192 + slab * 1024, 1024), 1024)
        return pltpu.make_async_copy(grid_ref.at[rows], out_ref.at[rows], sem.at[a, slab])

    def leave(slab):
        for a in range(2):
            outward(a, slab).start()
        return slab + 1

    def after(done, slab):
        return lax.while_loop(
            lambda at: (at < 8) & (list_ref[2 + jnp.minimum(at, 7)] <= done), leave, slab
        )

    slab = add_listed(
        direct(list_ref), list_ref[0], SLOTS, data_ref, grid_ref, TX, GROUP_LISTED, after=after
    )
    lax.while_loop(lambda at: at < 8, leave, slab)
    for slab in range(8):
        for a in range(2):
            outward(a, slab).wait()


def spread_round(head_ref, data_ref, from_ref, grid_ref, row_ref, tile_ref, sem):
    copy = pltpu.make_async_copy(from_ref, grid_ref, sem)
    copy.start()
    copy.wait()
    held = list_headed(head_ref, row_ref, tile_ref, ROOM, 16)
    add_listed(listed(row_ref, tile_ref), held, ROOM, data_ref, grid_ref, TX, GROUP)


def quarters(re, im):
    s02r, s02i = re[0] + re[2], im[0] + im[2]
    d02r, d02i = re[0] - re[2], im[0] - im[2]
    s13r, s13i = re[1] + re[3], im[1] + im[3]
    d13r, d13i = re[1] - re[3], im[1] - im[3]
    return [
        (s02r + s13r, s02i + s13i),
        (d02r - d13i, d02i + d13r),
        (s02r - s13r, s02i - s13i),
        (d02r + d13i, d02i - d13r),
    ]


def three_pass(high, low, value):
    top, rest = halves(value)

    def dot(a, b):
        return jnp.dot(a, b, preferred_element_type=jnp.float32)

    return dot(high, top) + (dot(high, rest) + dot(low, top))


def spread_and_turn(
    list_ref, head_ref, data_ref, high_ref, low_ref, from_ref, out_ref,
    grid_ref, sent_ref, row_ref, tile_ref, ends_ref, next_ref, sem, out_sem,
):
    def inward(a, slab):
        rows = pl.ds(pl.multiple_of(a * 512 + slab * 64, 64), 64)
        return pltpu.make_async_copy(
            from_ref.at[rows], grid_ref.at[rows, pl.ds(0, TX), :], sem.at[a, slab]
        )

    def arrive(slab):
        for a in range(2):
            inward(a, slab).wait()
        return slab + 1

    for slab in range(8):
        for a in range(2):
            inward(a, slab).start()
    held = list_strays(head_ref, row_ref, tile_ref, ends_ref, next_ref)
    flat = grid_ref.reshape(1024 * DEPTH, CAP)
    sent = sent_ref.reshape(128 * WIDE, CAP)

    def before(need, slab):
        return lax.while_loop(
            lambda at: (at < 8) & ((at == 0) | (ends_ref[jnp.maximum(at - 1, 0)] < need)),
            arrive,
            slab,
        )

    slab = add_listed(
        listed(row_ref, tile_ref), held, STRAYS, data_ref, flat, DEPTH, GROUP, before=before
    )
    lax.while_loop(lambda at: at < 8, arrive, slab)

    def columns(n, carry):
        j = 2 * n

        def plane(a, q):
            return jnp.concatenate(
                [
                    flat[pl.ds((a * 512 + q * 128) * DEPTH + j + u, 128, stride=DEPTH), :]
                    for u in range(2)
                ],
                axis=1,
            )

        re = [plane(0, q) for q in range(4)]
        im = [plane(1, q) for q in range(4)]
        for r, (real, imag) in enumerate(quarters(re, im)):
            turned = three_pass(high_ref[r], low_ref[r], jnp.concatenate([real, imag], axis=0))
            for a in range(2):
                for u in range(2):
                    sent[pl.ds(r * 32 + a * 16 + j + u, 128, stride=WIDE), :] = turned[
                        a * 128 : (a + 1) * 128, u * 128 : (u + 1) * 128
                    ]
        return carry

    def outward(n):
        return pltpu.make_async_copy(sent_ref.at[:, n], out_ref.at[:, n], out_sem.at[n])

    lax.fori_loop(0, 4, columns, 0)

    @pl.when(list_ref[1] > 0)
    def _():
        sent[pl.ds(0, 128, stride=WIDE), :] = jnp.full((128, CAP), MARK, jnp.float32)

    for n in range(8):
        outward(2 * n).start()
    lax.fori_loop(4, 8, columns, 0)
    for n in range(8):
        outward(2 * n + 1).start()
    for n in range(16):
        outward(n).wait()


def turn_planes(data_ref, high_ref, low_ref, y_ref, out_ref, mark_ref, rows_ref, left_ref):
    @pl.when(pl.program_id(0) == 0)
    def _():
        most = data_ref[0, 0, :, 0, 0, 0]
        for n in range(1, 16):
            most = jnp.maximum(most, data_ref[n // 4, n % 4, :, 0, 0, 0])
        mark_ref[0] = (jnp.max(most) > 0.1 * MARK).astype(jnp.int32)

    def plane(c, bx, by):
        return data_ref[bx, by, :, 0, c].reshape(128, CAP)

    for pair in range(2):
        ys = (2 * pair, 2 * pair + 1)
        re = [jnp.concatenate([plane(0, bx, by) for by in ys], axis=1) for bx in range(4)]
        im = [jnp.concatenate([plane(1, bx, by) for by in ys], axis=1) for bx in range(4)]
        for r, (real, imag) in enumerate(quarters(re, im)):
            turned = three_pass(high_ref[r], low_ref[r], jnp.concatenate([real, imag], axis=0))
            for a in range(2):
                for u in range(2):
                    start = (a * 4 + ys[u]) * GRID + r
                    rows_ref[pl.ds(start, 128, stride=4), :] = turned[
                        a * 128 : (a + 1) * 128, u * 128 : (u + 1) * 128
                    ]
    for n in range(8):
        left_ref[:, n * 128 : (n + 1) * 128] = rows_ref[n * GRID : (n + 1) * GRID, :].astype(
            jnp.bfloat16
        )
    for n in range(4):
        out_ref[n // 2, 0, :, (n % 2) * 256 : (n % 2 + 1) * 256] = jnp.dot(
            left_ref[...], y_ref[:, n * 256 : (n + 1) * 256], preferred_element_type=jnp.float32
        )


def smem():
    return pl.BlockSpec(memory_space=pltpu.SMEM)


def vmem():
    return pl.BlockSpec(memory_space=pltpu.VMEM)


def params(name):
    return pltpu.CompilerParams(vmem_limit_bytes=VMEM_MIB.get(name, 40) * MIB)


def swap(array, axis):
    return lax.all_to_all(array, axis, split_axis=0, concat_axis=0, tiled=True)


def call(kernel, out_shape, in_specs, out_specs, **options):
    return pl.pallas_call(
        kernel,
        out_shape=out_shape,
        in_specs=in_specs,
        out_specs=out_specs,
        compiler_params=params(kernel.__name__),
        name=kernel.__name__,
        **options,
    )


def anywhere():
    return pl.BlockSpec(memory_space=pl.ANY)


def large():
    return pl.BlockSpec(memory_space=pl.ANY)


def rows_of(rows):
    return jax.ShapeDtypeStruct((rows, CAP), jnp.float32)


def ints(count):
    return jax.ShapeDtypeStruct((count,), jnp.int32)


def body(z_high, z_low, x_high, x_low, y_table, spots, values, dest_brick, dest_tile, live_count):
    points = (
        dest_brick.reshape(256),
        dest_tile[0],
        live_count[0],
        spots[0].transpose(1, 0, 2),
        values[0],
    )

    def finish(blocks, heads, data, grid):
        columns = call(
            spread_and_turn,
            jax.ShapeDtypeStruct((128, 16, 8, CAP), jnp.float32),
            [smem(), smem(), vmem(), vmem(), vmem(), anywhere()],
            large(),
            scratch_shapes=[
                pltpu.VMEM((1024, DEPTH, CAP), jnp.float32),
                pltpu.VMEM((128, WIDE // 8, 8, CAP), jnp.float32),
                *[pltpu.SMEM((n,), jnp.int32) for n in (8 * STRAYS, 8 * STRAYS, 8, 8)],
                pltpu.SemaphoreType.DMA((2, 8)),
                pltpu.SemaphoreType.DMA((16,)),
            ],
        )(blocks, heads, data, z_high, z_low, grid.reshape(1024, TX, CAP))
        planes = swap(columns.reshape(128, 4, 2, TX, CAP), AXES).reshape(4, 4, 8, 4, 2, TX, CAP)
        return call(
            turn_planes,
            (jax.ShapeDtypeStruct((2, 4, GRID, GRID), jnp.float32), ints(1)),
            [
                pl.BlockSpec((4, 4, 8, 1, 2, TX, CAP), lambda q: (0, 0, 0, q, 0, 0, 0)),
                vmem(),
                vmem(),
                vmem(),
            ],
            (pl.BlockSpec((2, 1, GRID, GRID), lambda q: (0, q, 0, 0)), smem()),
            grid=(4,),
            scratch_shapes=[
                pltpu.VMEM((8 * GRID, CAP), jnp.float32),
                pltpu.VMEM((GRID, 2 * GRID), jnp.bfloat16),
            ],
        )(planes, x_high, x_low, y_table)

    me = lax.axis_index("gz").astype(jnp.int32).reshape(1)
    sent = call(
        pack_blocks,
        rows_of(128 * 16),
        [smem()] * 4 + [vmem()] * 2,
        vmem(),
        scratch_shapes=[pltpu.SMEM((n,), jnp.int32) for n in (256, 264, 128, 16)],
    )(me, *points)
    held = swap(sent.reshape(128, 16, CAP), AXES)
    heads = held[:, 15, :SLOTS].astype(jnp.int32).reshape(128 * SLOTS)
    held = held.reshape(128 * 16, CAP)
    strays, blocks = call(
        sort_blocks,
        (rows_of(8 * ROWS_S), ints(LIST)),
        [smem(), smem(), vmem()],
        (vmem(), smem()),
        scratch_shapes=[pltpu.SMEM((8,), jnp.int32)],
    )(me, heads, held)
    strays = swap(strays.reshape(8, ROWS_S, CAP), "gz")
    grid = call(
        spread_direct,
        rows_of(16384),
        [smem(), vmem()],
        large(),
        scratch_shapes=[pltpu.VMEM((16384, CAP), jnp.float32), pltpu.SemaphoreType.DMA((2, 8))],
        cost_estimate=pl.CostEstimate(flops=3 * 10**10, bytes_accessed=10**8, transcendentals=0),
    )(blocks, held)
    stray_heads = strays[:, 5 * STRAYS].astype(jnp.int32)
    density, mark = finish(blocks, stray_heads, strays.reshape(8 * ROWS_S, CAP), grid)

    def general(state):
        _, again, *given = lax.optimization_barrier((*state, *points))
        parts = call(
            pack_bricks,
            rows_of(16 * ROWS1),
            [smem()] * 3 + [vmem()] * 2,
            vmem(),
            scratch_shapes=[pltpu.SMEM((16,), jnp.int32)],
        )(*given)
        parts = swap(parts.reshape(16, ROWS1, CAP), "brick")
        head = parts[:, 5 * PER_DEST].astype(jnp.int32)
        parts = parts.reshape(16 * ROWS1, CAP)

        def another(inner):
            turn, _, total = inner
            packed = call(
                pack_tiles,
                rows_of(8 * ROWS2),
                [smem(), smem(), vmem()],
                vmem(),
                scratch_shapes=[pltpu.SMEM((8,), jnp.int32)],
            )(turn, head, parts)
            blocks = swap(packed.reshape(8, ROWS2, CAP), "gz")
            told = blocks[:, 5 * ROOM : 5 * ROOM + 2].astype(jnp.int32)
            total = call(
                spread_round,
                rows_of(16384),
                [smem(), vmem(), anywhere()],
                vmem(),
                scratch_shapes=[
                    pltpu.SMEM((8 * ROOM,), jnp.int32),
                    pltpu.SMEM((8 * ROOM,), jnp.int32),
                    pltpu.SemaphoreType.DMA,
                ],
            )(told[:, 0], blocks.reshape(8 * ROWS2, CAP), total)
            return turn + 1, ((jnp.max(told[:, 1]) + ROOM - 1) // ROOM).reshape(1), total

        _, _, total = lax.while_loop(
            lambda inner: inner[0][0] < inner[1][0],
            another,
            (
                jnp.zeros((1,), jnp.int32),
                jnp.ones((1,), jnp.int32),
                jnp.zeros((16384, CAP), jnp.float32),
            ),
        )
        none = jnp.zeros((8, CAP), jnp.int32)
        return finish(
            jnp.zeros((LIST,), jnp.int32),
            none,
            jnp.zeros((8 * ROWS_S, CAP), jnp.float32),
            total,
        )

    density, _ = lax.while_loop(lambda state: state[1][0] > 0, general, (density, mark))
    return density


def solution(mesh):
    in_specs = (
        P("gz", "brick", None, None),
        P("gz", "brick", None, None),
        P("gz", "brick", None),
        P("gz", "brick"),
        P("gz", "brick"),
    )
    out_specs = P(None, AXES, None, None)
    inverse = 1.0 / correction_of(GRID)
    z_high, z_low = quarter_tables(inverse * GRID ** (-1.5))
    x_high, x_low = quarter_tables(inverse)
    y_table = full_table(inverse)

    def whole(*args):
        tables = [jnp.asarray(t) for t in (z_high, z_low, x_high, x_low, y_table)]
        return jax.shard_map(
            functools.partial(body),
            mesh=mesh,
            in_specs=(P(),) * 5 + in_specs,
            out_specs=out_specs,
            check_vma=False,
        )(*tables, *args)

    return whole
```

```python
import functools
import math

import jax
import jax.numpy as jnp
import ml_dtypes
import numpy as np
from jax import lax
from jax.experimental import pallas as pl
from jax.experimental.pallas import tpu as pltpu
from jax.sharding import PartitionSpec as P

GRID = 512
TX = 16
TZ = 4
CAP = 128
AXES = ("brick", "gz")
PER_DEST = 24
ROWS1 = 5 * PER_DEST + 8
ROOM = 80
ROWS2 = 5 * ROOM + 8
LAST = 127
SLOTS = 3
STRAYS = 32
ROWS_S = 5 * STRAYS + 8
MARK = 1e30
GROUP = 32
LISTED = 16
STRAYED = LISTED + 392
LIST = STRAYED + 392
DEPTH = 24
WIDE = 136
MIB = 1024 * 1024
VMEM_MIB = {
    "pack_blocks": 8,
    "sort_blocks": 8,
    "spread_direct": 54,
    "spread_and_turn": 54,
    "turn_planes": 28,
}


def correction_of(length):
    places = np.arange(length)
    shifted = np.where(places < length // 2, places, places - length)
    nodes = np.arange(-63, 64)
    weights = np.maximum(0.0, 1.0 - (nodes / 32.0) ** 2 / 4.0) ** 10
    phases = shifted[:, None] * nodes[None, :] * (2.0 * math.pi / (32.0 * length))
    return np.sum(weights[None, :] * np.cos(phases), axis=1) / 32.0


def split(table):
    high = table.astype(np.float32).astype(ml_dtypes.bfloat16)
    low = (table - high.astype(np.float64)).astype(np.float32).astype(ml_dtypes.bfloat16)
    return high, low


def quarter_tables(scale):
    k, b = np.arange(128)[:, None], np.arange(128)[None, :]
    out = []
    for r in range(4):
        turned = (b * (4 * k + r)) % GRID
        angle = turned * (2.0 * math.pi / GRID)
        gain = scale[4 * np.arange(128) + r][:, None]
        c, s = np.cos(angle) * gain, np.sin(angle) * gain
        out.append(np.block([[c, -s], [s, c]]))
    return split(np.stack(out))


def full_table(scale):
    y, k = np.arange(GRID)[:, None], np.arange(GRID)[None, :]
    angle = (y * k % GRID) * (2.0 * math.pi / GRID)
    c, s = np.cos(angle) * scale[None, :], np.sin(angle) * scale[None, :]
    return np.block([[c, s], [-s, c]]).astype(np.float32).astype(ml_dtypes.bfloat16)


def lanes():
    return lax.broadcasted_iota(jnp.int32, (1, CAP), 1)


def pack_blocks(
    me_ref, brick_ref, tile_ref, live_ref, spots_ref, values_ref, out_ref,
    place_ref, left_ref, count_ref, turn_ref,
):
    lane = lanes()

    def clear(k, carry):
        count_ref[k] = 0
        out_ref[pl.ds(k * 16 + 15, 1), :] = jnp.full((1, CAP), -1.0, jnp.float32)
        return carry

    lax.fori_loop(0, 128, clear, 0, unroll=8)
    for b in range(16):
        turn_ref[b] = me_ref[0]

    def place(i, left):
        key = brick_ref[i] * 8 + lax.shift_right_logical(tile_ref[i], 4)
        count = count_ref[key]
        place_ref[i] = key * 16 + count
        count_ref[key] = jnp.minimum(count + 1, SLOTS)
        left_ref[left] = i
        return left + (count >= SLOTS).astype(jnp.int32)

    strays = lax.fori_loop(0, 256, place, 0, unroll=16)

    def stray(n, carry):
        i = left_ref[n]
        b = brick_ref[i]
        turn = lax.while_loop(
            lambda p: count_ref[b * 8 + (p & 7)] >= SLOTS, lambda p: p + 1, turn_ref[b]
        )
        key = b * 8 + (turn & 7)
        place_ref[i] = key * 16 + count_ref[key]
        count_ref[key] = count_ref[key] + 1
        turn_ref[b] = turn
        return carry

    lax.fori_loop(0, strays, stray, 0)

    def move(i, carry):
        row = place_ref[i]
        slot = row & 15
        for d in range(3):
            out_ref[pl.ds(row + d * SLOTS, 1), :] = spots_ref[d, pl.ds(i, 1), :]
        live = lane < live_ref[i]
        for d in range(2):
            out_ref[pl.ds(row + (3 + d) * SLOTS, 1), :] = jnp.where(
                live, values_ref[i, d : d + 1, :], 0.0
            )
        head = pl.ds(row - slot + 15, 1)
        out_ref[head, :] = jnp.where(lane == slot, tile_ref[i].astype(jnp.float32), out_ref[head, :])
        return carry

    lax.fori_loop(0, 256, move, 0, unroll=8)


def sort_blocks(me_ref, head_ref, data_ref, out_ref, list_ref, count_ref):
    lane = lanes()
    me = me_ref[0]
    for t in range(8):
        count_ref[t] = 0
        out_ref[t * ROWS_S + 5 * STRAYS : (t + 1) * ROWS_S, :] = jnp.zeros((8, CAP), jnp.float32)

    def look(n, found):
        own, strays = found
        source = (n & 15) * 8 + lax.shift_right_logical(n, 4)
        for c in range(SLOTS):
            tile = head_ref[source * SLOTS + c]
            straight = lax.shift_right_arithmetic(tile, 4) == me
            at = jnp.where(straight, LISTED + own, STRAYED + strays)
            list_ref[at] = (source * 16 + c) * 128 + tile
            own = own + straight.astype(jnp.int32)
            strays = strays + ((tile >= 0) & ~straight).astype(jnp.int32)
        list_ref[2 + lax.shift_right_logical(n, 4)] = own
        return own, strays

    own, strays = lax.fori_loop(0, 128, look, (0, 0), unroll=4)

    def forward(n, carry):
        code = list_ref[STRAYED + n]
        row = lax.shift_right_logical(code, 7)
        tile = code & 127
        tx = lax.shift_right_logical(tile, 4)
        k = count_ref[tx]
        count_ref[tx] = k + 1
        k = jnp.minimum(k, STRAYS - 1)
        for d in range(5):
            out_ref[pl.ds(tx * ROWS_S + d * STRAYS + k, 1), :] = data_ref[
                pl.ds(row + d * SLOTS, 1), :
            ]
        head = pl.ds(tx * ROWS_S + 5 * STRAYS, 1)
        depth = (row & 112) + (tile & 15)
        out_ref[head, :] = jnp.where(lane == k, depth.astype(jnp.float32), out_ref[head, :])
        return carry

    lax.fori_loop(0, strays, forward, 0)
    most = count_ref[0]
    for t in range(8):
        row = t * ROWS_S + 5 * STRAYS
        count = count_ref[t]
        most = jnp.maximum(most, count)
        sent = jnp.minimum(count, STRAYS).astype(jnp.float32)
        out_ref[row : row + 1, :] = jnp.where(lane == LAST, sent, out_ref[row : row + 1, :])
    list_ref[0] = own
    list_ref[1] = (most > STRAYS).astype(jnp.int32)


def pack_bricks(brick_ref, tile_ref, live_ref, spots_ref, values_ref, out_ref, count_ref):
    lane = lanes()
    for b in range(16):
        count_ref[b] = 0
        out_ref[b * ROWS1 + 5 * PER_DEST : (b + 1) * ROWS1, :] = jnp.zeros((8, CAP), jnp.float32)

    def step(i, tally):
        b = brick_ref[i]
        r = count_ref[b]
        count_ref[b] = r + 1
        base = b * ROWS1
        for d in range(3):
            out_ref[pl.ds(base + d * PER_DEST + r, 1), :] = spots_ref[d, pl.ds(i, 1), :]
        live = lane < live_ref[i]
        for d in range(2):
            out_ref[pl.ds(base + (3 + d) * PER_DEST + r, 1), :] = jnp.where(
                live, values_ref[i, d : d + 1, :], 0.0
            )
        head = pl.ds(base + 5 * PER_DEST, 1)
        tile = tile_ref[i]
        out_ref[head, :] = jnp.where(lane == r, tile.astype(jnp.float32), out_ref[head, :])
        key = b * 8 + lax.shift_right_logical(tile, 4)
        return tally + jnp.where(lane == key, 1.0, 0.0)

    tally = lax.fori_loop(0, 256, step, jnp.zeros((1, CAP), jnp.float32), unroll=4)
    for b in range(16):
        row = b * ROWS1 + 5 * PER_DEST
        total = count_ref[b].astype(jnp.float32)
        out_ref[row : row + 1, :] = jnp.where(lane == LAST, total, out_ref[row : row + 1, :])
        out_ref[row + 1 : row + 2, :] = tally


def pack_tiles(round_ref, head_ref, data_ref, out_ref, count_ref):
    lane = lanes()
    first = round_ref[0] * ROOM
    for t in range(8):
        count_ref[t] = 0
        out_ref[t * ROWS2 + 5 * ROOM : (t + 1) * ROWS2, :] = jnp.zeros((8, CAP), jnp.float32)
    spare = 5 * ROOM + 7

    def source(s, carry):
        held = head_ref[s, LAST]

        def step(i, inner):
            tile = head_ref[s, i]
            live = i < held
            tx = lax.shift_right_logical(tile, 4)
            place = count_ref[tx]
            count_ref[tx] = place + live.astype(jnp.int32)
            k = place - first
            good = live & (k >= 0) & (k < ROOM)
            base = tx * ROWS2
            for d in range(5):
                row = jnp.where(good, base + d * ROOM + k, spare)
                out_ref[pl.ds(row, 1), :] = data_ref[pl.ds(s * ROWS1 + d * PER_DEST + i, 1), :]
            head = pl.ds(base + 5 * ROOM, 1)
            depth = (tile & 15).astype(jnp.float32)
            spot = jnp.where(good, k, -1)
            out_ref[head, :] = jnp.where(lane == spot, depth, out_ref[head, :])
            return inner

        return lax.fori_loop(0, PER_DEST, step, carry, unroll=4)

    lax.fori_loop(0, 16, source, 0)
    tally = data_ref[5 * PER_DEST + 1 : 5 * PER_DEST + 2, :]
    for s in range(1, 16):
        row = s * ROWS1 + 5 * PER_DEST + 1
        tally = tally + data_ref[row : row + 1, :]
    for t in range(8):
        row = t * ROWS2 + 5 * ROOM
        count = count_ref[t]
        sent = jnp.clip(count - first, 0, ROOM).astype(jnp.float32)
        out_ref[row : row + 1, :] = jnp.where(lane == LAST, sent, out_ref[row : row + 1, :])
        out_ref[row + 1 : row + 2, :] = tally


def phi10(t):
    square = t * t
    fourth = square * square
    return fourth * fourth * square


def weights_at(cells, position):
    half = cells - 0.5 * position
    return phi10(jnp.maximum(0.0, 1.0 - half * half))


def halves(value):
    high = value.astype(jnp.bfloat16)
    return high, (value - high.astype(jnp.float32)).astype(jnp.bfloat16)


def block_cells(data_ref, row, step, scale):
    def at(d):
        return data_ref[pl.ds(row + d * step, 1), :]

    pos_x = -1.0 + (TX + 2) * at(0)
    pos_y = -1.0 + (CAP + 2) * at(1)
    pos_z = -1.0 + (TZ + 2) * at(2)
    half_cells = 0.5 * lax.broadcasted_iota(jnp.int32, (TX, CAP), 0).astype(jnp.float32)
    wx = weights_at(half_cells, pos_x).astype(jnp.bfloat16).astype(jnp.float32)
    wz = weights_at(half_cells[:8], pos_z)
    parts = []
    for d in (3, 4):
        wzv = wz * (at(d) * scale)
        for l in range(TZ):
            parts.append(wx * wzv[l : l + 1, :])
    left_high, left_low = halves(jnp.concatenate(parts, axis=0))
    first = jnp.floor(pos_y) - 1.0
    near_high, near_low = halves(weights_at(half_cells[:8], pos_y - first))
    cells = lax.broadcasted_iota(jnp.int32, (CAP, CAP), 0).astype(jnp.float32)
    place = cells.astype(jnp.bfloat16) - first.astype(jnp.bfloat16)
    high = jnp.zeros((CAP, CAP), jnp.bfloat16)
    low = high
    for k in range(4):
        here = place == jnp.bfloat16(k)
        high = jnp.where(here, near_high[k : k + 1, :], high)
        low = jnp.where(here, near_low[k : k + 1, :], low)
    return lax.dot_general(
        jnp.concatenate([left_high, left_high, left_low], axis=1),
        jnp.concatenate([high, low, high], axis=1),
        (((1,), (1,)), ((), ())),
        preferred_element_type=jnp.float32,
    )


def add_listed(find, held, step, data_ref, grid_ref, depth, size, before=None, after=None):
    def group(n, carry):
        if before is not None:
            carry = before(jnp.minimum((n + 1) * size, held), carry)
        found = []
        for u in range(size):
            i = n * size + u
            live = i < held
            row, tile = find(jnp.where(live, i, 0))
            scale = jnp.where(live, 1.0, 0.0).astype(jnp.float32)
            found.append((tile, block_cells(data_ref, row, step, scale)))
        for tile, cells in found:
            for a in range(2):
                for l in range(TZ):
                    start = (a * 512 + tile * TZ + l) * depth
                    rows = pl.ds(pl.multiple_of(start, 8), TX)
                    part = (a * TZ + l) * TX
                    grid_ref[rows, :] += cells[part : part + TX]
        return carry if after is None else after((n + 1) * size, carry)

    return lax.fori_loop(0, (held + size - 1) // size, group, 0)


def direct(list_ref):
    def find(i):
        code = list_ref[LISTED + i]
        row = lax.shift_right_logical(code, 7)
        return row, (row & 112) + (code & 15)

    return find


def listed(row_ref, tile_ref):
    return lambda i: (row_ref[i], tile_ref[i])


def list_headed(head_ref, row_ref, tile_ref, room, base):
    def source(g, total):
        def entry(i, at):
            row_ref[at] = g * (5 * room + 8) + i
            tile_ref[at] = head_ref[g, i] + base * g
            return at + 1

        return lax.fori_loop(0, head_ref[g, LAST], entry, total)

    return lax.fori_loop(0, 8, source, 0)


def clear_grid(grid_ref):
    def clear(i, carry):
        grid_ref[pl.ds(pl.multiple_of(i * 64, 64), 64), :] = jnp.zeros((64, CAP), jnp.float32)
        return carry

    lax.fori_loop(0, 16384 // 64, clear, 0, unroll=4)


def list_strays(head_ref, row_ref, tile_ref, ends_ref, next_ref):
    for h in range(8):
        next_ref[h] = 0

    def slab(g, total):
        def source(h, so_far):
            held = head_ref[h, LAST]

            def more(state):
                i, _ = state
                return (i < held) & (lax.shift_right_logical(head_ref[h, i & 63], 4) == g)

            def entry(state):
                i, at = state
                row_ref[at] = h * ROWS_S + i
                tile_ref[at] = head_ref[h, i]
                return i + 1, at + 1

            i, so_far = lax.while_loop(more, entry, (next_ref[h], so_far))
            next_ref[h] = i
            return so_far

        total = lax.fori_loop(0, 8, source, total)
        ends_ref[g] = total
        return total

    return lax.fori_loop(0, 8, slab, 0)


def spread_direct(list_ref, data_ref, out_ref, grid_ref, sem):
    clear_grid(grid_ref)

    def outward(a, slab):
        rows = pl.ds(pl.multiple_of(a * 8192 + slab * 1024, 1024), 1024)
        return pltpu.make_async_copy(grid_ref.at[rows], out_ref.at[rows], sem.at[a, slab])

    def leave(slab):
        for a in range(2):
            outward(a, slab).start()
        return slab + 1

    def after(done, slab):
        return lax.while_loop(
            lambda at: (at < 8) & (list_ref[2 + jnp.minimum(at, 7)] <= done), leave, slab
        )

    slab = add_listed(
        direct(list_ref), list_ref[0], SLOTS, data_ref, grid_ref, TX, GROUP, after=after
    )
    lax.while_loop(lambda at: at < 8, leave, slab)
    for slab in range(8):
        for a in range(2):
            outward(a, slab).wait()


def spread_round(head_ref, data_ref, from_ref, grid_ref, row_ref, tile_ref, sem):
    copy = pltpu.make_async_copy(from_ref, grid_ref, sem)
    copy.start()
    copy.wait()
    held = list_headed(head_ref, row_ref, tile_ref, ROOM, 16)
    add_listed(listed(row_ref, tile_ref), held, ROOM, data_ref, grid_ref, TX, GROUP)


def quarters(re, im):
    s02r, s02i = re[0] + re[2], im[0] + im[2]
    d02r, d02i = re[0] - re[2], im[0] - im[2]
    s13r, s13i = re[1] + re[3], im[1] + im[3]
    d13r, d13i = re[1] - re[3], im[1] - im[3]
    return [
        (s02r + s13r, s02i + s13i),
        (d02r - d13i, d02i + d13r),
        (s02r - s13r, s02i - s13i),
        (d02r + d13i, d02i - d13r),
    ]


def three_pass(high, low, value):
    top, rest = halves(value)

    def dot(a, b):
        return jnp.dot(a, b, preferred_element_type=jnp.float32)

    return (dot(high, top) + dot(high, rest)) + dot(low, top)


def spread_and_turn(
    list_ref, head_ref, data_ref, high_ref, low_ref, from_ref, out_ref,
    grid_ref, sent_ref, row_ref, tile_ref, ends_ref, next_ref, sem, out_sem,
):
    def inward(a, slab):
        rows = pl.ds(pl.multiple_of(a * 512 + slab * 64, 64), 64)
        return pltpu.make_async_copy(
            from_ref.at[rows], grid_ref.at[rows, pl.ds(0, TX), :], sem.at[a, slab]
        )

    def arrive(slab):
        for a in range(2):
            inward(a, slab).wait()
        return slab + 1

    for slab in range(8):
        for a in range(2):
            inward(a, slab).start()
    held = list_strays(head_ref, row_ref, tile_ref, ends_ref, next_ref)
    flat = grid_ref.reshape(1024 * DEPTH, CAP)
    sent = sent_ref.reshape(128 * WIDE, CAP)

    def before(need, slab):
        return lax.while_loop(
            lambda at: (at < 8) & ((at == 0) | (ends_ref[jnp.maximum(at - 1, 0)] < need)),
            arrive,
            slab,
        )

    slab = add_listed(
        listed(row_ref, tile_ref), held, STRAYS, data_ref, flat, DEPTH, GROUP, before=before
    )
    lax.while_loop(lambda at: at < 8, arrive, slab)

    def columns(n, carry):
        j = 2 * n

        def plane(a, q):
            return jnp.concatenate(
                [
                    flat[pl.ds((a * 512 + q * 128) * DEPTH + j + u, 128, stride=DEPTH), :]
                    for u in range(2)
                ],
                axis=1,
            )

        re = [plane(0, q) for q in range(4)]
        im = [plane(1, q) for q in range(4)]
        for r, (real, imag) in enumerate(quarters(re, im)):
            turned = three_pass(high_ref[r], low_ref[r], jnp.concatenate([real, imag], axis=0))
            for a in range(2):
                for u in range(2):
                    sent[pl.ds(r * 32 + a * 16 + j + u, 128, stride=WIDE), :] = turned[
                        a * 128 : (a + 1) * 128, u * 128 : (u + 1) * 128
                    ]
        return carry

    def outward(n):
        return pltpu.make_async_copy(sent_ref.at[:, n], out_ref.at[:, n], out_sem.at[n])

    lax.fori_loop(0, 4, columns, 0, unroll=2)

    @pl.when(list_ref[1] > 0)
    def _():
        sent[pl.ds(0, 128, stride=WIDE), :] = jnp.full((128, CAP), MARK, jnp.float32)

    for n in range(8):
        outward(2 * n).start()
    lax.fori_loop(4, 8, columns, 0, unroll=2)
    for n in range(8):
        outward(2 * n + 1).start()
    for n in range(16):
        outward(n).wait()


def turn_planes(data_ref, high_ref, low_ref, y_ref, out_ref, mark_ref, rows_ref, left_ref):
    @pl.when(pl.program_id(0) == 0)
    def _():
        most = data_ref[0, 0, :, 0, 0, 0]
        for n in range(1, 16):
            most = jnp.maximum(most, data_ref[n // 4, n % 4, :, 0, 0, 0])
        mark_ref[0] = (jnp.max(most) > 0.1 * MARK).astype(jnp.int32)

    def plane(c, bx, by):
        return data_ref[bx, by, :, 0, c].reshape(128, CAP)

    for pair in range(2):
        ys = (2 * pair, 2 * pair + 1)
        re = [jnp.concatenate([plane(0, bx, by) for by in ys], axis=1) for bx in range(4)]
        im = [jnp.concatenate([plane(1, bx, by) for by in ys], axis=1) for bx in range(4)]
        for r, (real, imag) in enumerate(quarters(re, im)):
            turned = three_pass(high_ref[r], low_ref[r], jnp.concatenate([real, imag], axis=0))
            for a in range(2):
                for u in range(2):
                    start = (a * 4 + ys[u]) * GRID + r
                    rows_ref[pl.ds(start, 128, stride=4), :] = turned[
                        a * 128 : (a + 1) * 128, u * 128 : (u + 1) * 128
                    ]
    for n in range(8):
        left_ref[:, n * 128 : (n + 1) * 128] = rows_ref[n * GRID : (n + 1) * GRID, :].astype(
            jnp.bfloat16
        )
    for n in range(4):
        out_ref[n // 2, 0, :, (n % 2) * 256 : (n % 2 + 1) * 256] = jnp.dot(
            left_ref[...], y_ref[:, n * 256 : (n + 1) * 256], preferred_element_type=jnp.float32
        )


def smem():
    return pl.BlockSpec(memory_space=pltpu.SMEM)


def vmem():
    return pl.BlockSpec(memory_space=pltpu.VMEM)


def params(name):
    return pltpu.CompilerParams(vmem_limit_bytes=VMEM_MIB.get(name, 40) * MIB)


def swap(array, axis):
    return lax.all_to_all(array, axis, split_axis=0, concat_axis=0, tiled=True)


def call(kernel, out_shape, in_specs, out_specs, **options):
    return pl.pallas_call(
        kernel,
        out_shape=out_shape,
        in_specs=in_specs,
        out_specs=out_specs,
        compiler_params=params(kernel.__name__),
        name=kernel.__name__,
        **options,
    )


def anywhere():
    return pl.BlockSpec(memory_space=pl.ANY)


def large():
    return pl.BlockSpec(memory_space=pl.ANY)


def rows_of(rows):
    return jax.ShapeDtypeStruct((rows, CAP), jnp.float32)


def ints(count):
    return jax.ShapeDtypeStruct((count,), jnp.int32)


def body(z_high, z_low, x_high, x_low, y_table, spots, values, dest_brick, dest_tile, live_count):
    points = (
        dest_brick.reshape(256),
        dest_tile[0],
        live_count[0],
        spots[0].transpose(1, 0, 2),
        values[0],
    )

    def finish(blocks, heads, data, grid):
        columns = call(
            spread_and_turn,
            jax.ShapeDtypeStruct((128, 16, 8, CAP), jnp.float32),
            [smem(), smem(), vmem(), vmem(), vmem(), anywhere()],
            large(),
            scratch_shapes=[
                pltpu.VMEM((1024, DEPTH, CAP), jnp.float32),
                pltpu.VMEM((128, WIDE // 8, 8, CAP), jnp.float32),
                *[pltpu.SMEM((n,), jnp.int32) for n in (8 * STRAYS, 8 * STRAYS, 8, 8)],
                pltpu.SemaphoreType.DMA((2, 8)),
                pltpu.SemaphoreType.DMA((16,)),
            ],
        )(blocks, heads, data, z_high, z_low, grid.reshape(1024, TX, CAP))
        planes = swap(columns.reshape(128, 4, 2, TX, CAP), AXES).reshape(4, 4, 8, 4, 2, TX, CAP)
        return call(
            turn_planes,
            (jax.ShapeDtypeStruct((2, 4, GRID, GRID), jnp.float32), ints(1)),
            [
                pl.BlockSpec((4, 4, 8, 1, 2, TX, CAP), lambda q: (0, 0, 0, q, 0, 0, 0)),
                vmem(),
                vmem(),
                vmem(),
            ],
            (pl.BlockSpec((2, 1, GRID, GRID), lambda q: (0, q, 0, 0)), smem()),
            grid=(4,),
            scratch_shapes=[
                pltpu.VMEM((8 * GRID, CAP), jnp.float32),
                pltpu.VMEM((GRID, 2 * GRID), jnp.bfloat16),
            ],
        )(planes, x_high, x_low, y_table)

    me = lax.axis_index("gz").astype(jnp.int32).reshape(1)
    sent = call(
        pack_blocks,
        rows_of(128 * 16),
        [smem()] * 4 + [vmem()] * 2,
        vmem(),
        scratch_shapes=[pltpu.SMEM((n,), jnp.int32) for n in (256, 264, 128, 16)],
    )(me, *points)
    held = swap(sent.reshape(128, 16, CAP), AXES)
    heads = held[:, 15, :SLOTS].astype(jnp.int32).reshape(128 * SLOTS)
    held = held.reshape(128 * 16, CAP)
    strays, blocks = call(
        sort_blocks,
        (rows_of(8 * ROWS_S), ints(LIST)),
        [smem(), smem(), vmem()],
        (vmem(), smem()),
        scratch_shapes=[pltpu.SMEM((8,), jnp.int32)],
    )(me, heads, held)
    strays = swap(strays.reshape(8, ROWS_S, CAP), "gz")
    grid = call(
        spread_direct,
        rows_of(16384),
        [smem(), vmem()],
        large(),
        scratch_shapes=[pltpu.VMEM((16384, CAP), jnp.float32), pltpu.SemaphoreType.DMA((2, 8))],
        cost_estimate=pl.CostEstimate(flops=3 * 10**10, bytes_accessed=10**8, transcendentals=0),
    )(blocks, held)
    stray_heads = strays[:, 5 * STRAYS].astype(jnp.int32)
    density, mark = finish(blocks, stray_heads, strays.reshape(8 * ROWS_S, CAP), grid)

    def general(state):
        _, again, *given = lax.optimization_barrier((*state, *points))
        parts = call(
            pack_bricks,
            rows_of(16 * ROWS1),
            [smem()] * 3 + [vmem()] * 2,
            vmem(),
            scratch_shapes=[pltpu.SMEM((16,), jnp.int32)],
        )(*given)
        parts = swap(parts.reshape(16, ROWS1, CAP), "brick")
        head = parts[:, 5 * PER_DEST].astype(jnp.int32)
        parts = parts.reshape(16 * ROWS1, CAP)

        def another(inner):
            turn, _, total = inner
            packed = call(
                pack_tiles,
                rows_of(8 * ROWS2),
                [smem(), smem(), vmem()],
                vmem(),
                scratch_shapes=[pltpu.SMEM((8,), jnp.int32)],
            )(turn, head, parts)
            blocks = swap(packed.reshape(8, ROWS2, CAP), "gz")
            told = blocks[:, 5 * ROOM : 5 * ROOM + 2].astype(jnp.int32)
            total = call(
                spread_round,
                rows_of(16384),
                [smem(), vmem(), anywhere()],
                vmem(),
                scratch_shapes=[
                    pltpu.SMEM((8 * ROOM,), jnp.int32),
                    pltpu.SMEM((8 * ROOM,), jnp.int32),
                    pltpu.SemaphoreType.DMA,
                ],
            )(told[:, 0], blocks.reshape(8 * ROWS2, CAP), total)
            return turn + 1, ((jnp.max(told[:, 1]) + ROOM - 1) // ROOM).reshape(1), total

        _, _, total = lax.while_loop(
            lambda inner: inner[0][0] < inner[1][0],
            another,
            (
                jnp.zeros((1,), jnp.int32),
                jnp.ones((1,), jnp.int32),
                jnp.zeros((16384, CAP), jnp.float32),
            ),
        )
        none = jnp.zeros((8, CAP), jnp.int32)
        return finish(
            jnp.zeros((LIST,), jnp.int32),
            none,
            jnp.zeros((8 * ROWS_S, CAP), jnp.float32),
            total,
        )

    density, _ = lax.while_loop(lambda state: state[1][0] > 0, general, (density, mark))
    return density


def solution(mesh):
    in_specs = (
        P("gz", "brick", None, None),
        P("gz", "brick", None, None),
        P("gz", "brick", None),
        P("gz", "brick"),
        P("gz", "brick"),
    )
    out_specs = P(None, AXES, None, None)
    inverse = 1.0 / correction_of(GRID)
    z_high, z_low = quarter_tables(inverse * GRID ** (-1.5))
    x_high, x_low = quarter_tables(inverse)
    y_table = full_table(inverse)

    def whole(*args):
        tables = [jnp.asarray(t) for t in (z_high, z_low, x_high, x_low, y_table)]
        return jax.shard_map(
            functools.partial(body),
            mesh=mesh,
            in_specs=(P(),) * 5 + in_specs,
            out_specs=out_specs,
            check_vma=False,
        )(*tables, *args)

    return whole
```

```python
import functools
import math

import jax
import jax.numpy as jnp
import ml_dtypes
import numpy as np
from jax import lax
from jax.experimental import pallas as pl
from jax.experimental.pallas import tpu as pltpu
from jax.sharding import PartitionSpec as P

GRID = 512
TX = 16
TZ = 4
CAP = 128
AXES = ("brick", "gz")
PER_DEST = 24
ROWS1 = 5 * PER_DEST + 8
ROOM = 80
ROWS2 = 5 * ROOM + 8
LAST = 127
SLOTS = 3
STRAYS = 32
ROWS_S = 5 * STRAYS + 8
MARK = 1e30
GROUP = 32
LISTED = 16
STRAYED = LISTED + 392
LIST = STRAYED + 392
DEPTH = 24
WIDE = 136
MIB = 1024 * 1024
VMEM_MIB = {
    "pack_blocks": 8,
    "sort_blocks": 8,
    "spread_direct": 54,
    "spread_and_turn": 54,
    "turn_planes": 28,
}


def correction_of(length):
    places = np.arange(length)
    shifted = np.where(places < length // 2, places, places - length)
    nodes = np.arange(-63, 64)
    weights = np.maximum(0.0, 1.0 - (nodes / 32.0) ** 2 / 4.0) ** 10
    phases = shifted[:, None] * nodes[None, :] * (2.0 * math.pi / (32.0 * length))
    return np.sum(weights[None, :] * np.cos(phases), axis=1) / 32.0


def split(table):
    high = table.astype(np.float32).astype(ml_dtypes.bfloat16)
    low = (table - high.astype(np.float64)).astype(np.float32).astype(ml_dtypes.bfloat16)
    return high, low


def quarter_tables(scale):
    k, b = np.arange(128)[:, None], np.arange(128)[None, :]
    out = []
    for r in range(4):
        turned = (b * (4 * k + r)) % GRID
        angle = turned * (2.0 * math.pi / GRID)
        gain = scale[4 * np.arange(128) + r][:, None]
        c, s = np.cos(angle) * gain, np.sin(angle) * gain
        out.append(np.block([[c, -s], [s, c]]))
    return split(np.stack(out))


def full_table(scale):
    y, k = np.arange(GRID)[:, None], np.arange(GRID)[None, :]
    angle = (y * k % GRID) * (2.0 * math.pi / GRID)
    c, s = np.cos(angle) * scale[None, :], np.sin(angle) * scale[None, :]
    return np.block([[c, s], [-s, c]]).astype(np.float32).astype(ml_dtypes.bfloat16)


def lanes():
    return lax.broadcasted_iota(jnp.int32, (1, CAP), 1)


def pack_blocks(
    me_ref, brick_ref, tile_ref, live_ref, spots_ref, values_ref, out_ref,
    place_ref, left_ref, count_ref, turn_ref,
):
    lane = lanes()

    def clear(k, carry):
        count_ref[k] = 0
        out_ref[pl.ds(k * 16 + 15, 1), :] = jnp.full((1, CAP), -1.0, jnp.float32)
        return carry

    lax.fori_loop(0, 128, clear, 0, unroll=8)
    for b in range(16):
        turn_ref[b] = me_ref[0]

    def place(i, left):
        key = brick_ref[i] * 8 + lax.shift_right_logical(tile_ref[i], 4)
        count = count_ref[key]
        place_ref[i] = key * 16 + count
        count_ref[key] = jnp.minimum(count + 1, SLOTS)
        left_ref[left] = i
        return left + (count >= SLOTS).astype(jnp.int32)

    strays = lax.fori_loop(0, 256, place, 0, unroll=16)

    def stray(n, carry):
        i = left_ref[n]
        b = brick_ref[i]
        turn = lax.while_loop(
            lambda p: count_ref[b * 8 + (p & 7)] >= SLOTS, lambda p: p + 1, turn_ref[b]
        )
        key = b * 8 + (turn & 7)
        place_ref[i] = key * 16 + count_ref[key]
        count_ref[key] = count_ref[key] + 1
        turn_ref[b] = turn
        return carry

    lax.fori_loop(0, strays, stray, 0)

    def move(i, carry):
        row = place_ref[i]
        slot = row & 15
        for d in range(3):
            out_ref[pl.ds(row + d * SLOTS, 1), :] = spots_ref[d, pl.ds(i, 1), :]
        live = lane < live_ref[i]
        for d in range(2):
            out_ref[pl.ds(row + (3 + d) * SLOTS, 1), :] = jnp.where(
                live, values_ref[i, d : d + 1, :], 0.0
            )
        head = pl.ds(row - slot + 15, 1)
        out_ref[head, :] = jnp.where(lane == slot, tile_ref[i].astype(jnp.float32), out_ref[head, :])
        return carry

    lax.fori_loop(0, 256, move, 0, unroll=8)


def sort_blocks(me_ref, head_ref, data_ref, out_ref, list_ref, count_ref):
    lane = lanes()
    me = me_ref[0]
    for t in range(8):
        count_ref[t] = 0
        out_ref[t * ROWS_S + 5 * STRAYS : (t + 1) * ROWS_S, :] = jnp.zeros((8, CAP), jnp.float32)

    def look(n, found):
        own, strays = found
        source = (n & 15) * 8 + lax.shift_right_logical(n, 4)
        for c in range(SLOTS):
            tile = head_ref[source * SLOTS + c]
            straight = lax.shift_right_arithmetic(tile, 4) == me
            at = jnp.where(straight, LISTED + own, STRAYED + strays)
            list_ref[at] = (source * 16 + c) * 128 + tile
            own = own + straight.astype(jnp.int32)
            strays = strays + ((tile >= 0) & ~straight).astype(jnp.int32)
        list_ref[2 + lax.shift_right_logical(n, 4)] = own
        return own, strays

    own, strays = lax.fori_loop(0, 128, look, (0, 0), unroll=8)

    def forward(n, carry):
        code = list_ref[STRAYED + n]
        row = lax.shift_right_logical(code, 7)
        tile = code & 127
        tx = lax.shift_right_logical(tile, 4)
        k = count_ref[tx]
        count_ref[tx] = k + 1
        k = jnp.minimum(k, STRAYS - 1)
        for d in range(5):
            out_ref[pl.ds(tx * ROWS_S + d * STRAYS + k, 1), :] = data_ref[
                pl.ds(row + d * SLOTS, 1), :
            ]
        head = pl.ds(tx * ROWS_S + 5 * STRAYS, 1)
        depth = (row & 112) + (tile & 15)
        out_ref[head, :] = jnp.where(lane == k, depth.astype(jnp.float32), out_ref[head, :])
        return carry

    lax.fori_loop(0, strays, forward, 0)
    most = count_ref[0]
    for t in range(8):
        row = t * ROWS_S + 5 * STRAYS
        count = count_ref[t]
        most = jnp.maximum(most, count)
        sent = jnp.minimum(count, STRAYS).astype(jnp.float32)
        out_ref[row : row + 1, :] = jnp.where(lane == LAST, sent, out_ref[row : row + 1, :])
    list_ref[0] = own
    list_ref[1] = (most > STRAYS).astype(jnp.int32)


def pack_bricks(brick_ref, tile_ref, live_ref, spots_ref, values_ref, out_ref, count_ref):
    lane = lanes()
    for b in range(16):
        count_ref[b] = 0
        out_ref[b * ROWS1 + 5 * PER_DEST : (b + 1) * ROWS1, :] = jnp.zeros((8, CAP), jnp.float32)

    def step(i, tally):
        b = brick_ref[i]
        r = count_ref[b]
        count_ref[b] = r + 1
        base = b * ROWS1
        for d in range(3):
            out_ref[pl.ds(base + d * PER_DEST + r, 1), :] = spots_ref[d, pl.ds(i, 1), :]
        live = lane < live_ref[i]
        for d in range(2):
            out_ref[pl.ds(base + (3 + d) * PER_DEST + r, 1), :] = jnp.where(
                live, values_ref[i, d : d + 1, :], 0.0
            )
        head = pl.ds(base + 5 * PER_DEST, 1)
        tile = tile_ref[i]
        out_ref[head, :] = jnp.where(lane == r, tile.astype(jnp.float32), out_ref[head, :])
        key = b * 8 + lax.shift_right_logical(tile, 4)
        return tally + jnp.where(lane == key, 1.0, 0.0)

    tally = lax.fori_loop(0, 256, step, jnp.zeros((1, CAP), jnp.float32), unroll=4)
    for b in range(16):
        row = b * ROWS1 + 5 * PER_DEST
        total = count_ref[b].astype(jnp.float32)
        out_ref[row : row + 1, :] = jnp.where(lane == LAST, total, out_ref[row : row + 1, :])
        out_ref[row + 1 : row + 2, :] = tally


def pack_tiles(round_ref, head_ref, data_ref, out_ref, count_ref):
    lane = lanes()
    first = round_ref[0] * ROOM
    for t in range(8):
        count_ref[t] = 0
        out_ref[t * ROWS2 + 5 * ROOM : (t + 1) * ROWS2, :] = jnp.zeros((8, CAP), jnp.float32)
    spare = 5 * ROOM + 7

    def source(s, carry):
        held = head_ref[s, LAST]

        def step(i, inner):
            tile = head_ref[s, i]
            live = i < held
            tx = lax.shift_right_logical(tile, 4)
            place = count_ref[tx]
            count_ref[tx] = place + live.astype(jnp.int32)
            k = place - first
            good = live & (k >= 0) & (k < ROOM)
            base = tx * ROWS2
            for d in range(5):
                row = jnp.where(good, base + d * ROOM + k, spare)
                out_ref[pl.ds(row, 1), :] = data_ref[pl.ds(s * ROWS1 + d * PER_DEST + i, 1), :]
            head = pl.ds(base + 5 * ROOM, 1)
            depth = (tile & 15).astype(jnp.float32)
            spot = jnp.where(good, k, -1)
            out_ref[head, :] = jnp.where(lane == spot, depth, out_ref[head, :])
            return inner

        return lax.fori_loop(0, PER_DEST, step, carry, unroll=4)

    lax.fori_loop(0, 16, source, 0)
    tally = data_ref[5 * PER_DEST + 1 : 5 * PER_DEST + 2, :]
    for s in range(1, 16):
        row = s * ROWS1 + 5 * PER_DEST + 1
        tally = tally + data_ref[row : row + 1, :]
    for t in range(8):
        row = t * ROWS2 + 5 * ROOM
        count = count_ref[t]
        sent = jnp.clip(count - first, 0, ROOM).astype(jnp.float32)
        out_ref[row : row + 1, :] = jnp.where(lane == LAST, sent, out_ref[row : row + 1, :])
        out_ref[row + 1 : row + 2, :] = tally


def phi10(t):
    square = t * t
    fourth = square * square
    return fourth * fourth * square


def weights_at(cells, position):
    half = cells - 0.5 * position
    return phi10(jnp.maximum(0.0, 1.0 - half * half))


def halves(value):
    high = value.astype(jnp.bfloat16)
    return high, (value - high.astype(jnp.float32)).astype(jnp.bfloat16)


def block_cells(data_ref, row, step, scale):
    def at(d):
        return data_ref[pl.ds(row + d * step, 1), :]

    pos_x = -1.0 + (TX + 2) * at(0)
    pos_y = -1.0 + (CAP + 2) * at(1)
    pos_z = -1.0 + (TZ + 2) * at(2)
    half_cells = 0.5 * lax.broadcasted_iota(jnp.int32, (TX, CAP), 0).astype(jnp.float32)
    wx = weights_at(half_cells, pos_x).astype(jnp.bfloat16).astype(jnp.float32)
    wz = weights_at(half_cells[:8], pos_z)
    parts = []
    for d in (3, 4):
        wzv = wz * (at(d) * scale)
        for l in range(TZ):
            parts.append(wx * wzv[l : l + 1, :])
    left_high, left_low = halves(jnp.concatenate(parts, axis=0))
    first = jnp.floor(pos_y) - 1.0
    near_high, near_low = halves(weights_at(half_cells[:8], pos_y - first))
    cells = lax.broadcasted_iota(jnp.int32, (CAP, CAP), 0).astype(jnp.float32)
    place = cells.astype(jnp.bfloat16) - first.astype(jnp.bfloat16)
    high = jnp.zeros((CAP, CAP), jnp.bfloat16)
    low = high
    for k in range(4):
        here = place == jnp.bfloat16(k)
        high = jnp.where(here, near_high[k : k + 1, :], high)
        low = jnp.where(here, near_low[k : k + 1, :], low)
    return lax.dot_general(
        jnp.concatenate([left_high, left_high, left_low], axis=1),
        jnp.concatenate([high, low, high], axis=1),
        (((1,), (1,)), ((), ())),
        preferred_element_type=jnp.float32,
    )


def add_listed(find, held, step, data_ref, grid_ref, depth, size, before=None, after=None):
    def group(n, carry):
        if before is not None:
            carry = before(jnp.minimum((n + 1) * size, held), carry)
        found = []
        for u in range(size):
            i = n * size + u
            live = i < held
            row, tile = find(jnp.where(live, i, 0))
            scale = jnp.where(live, 1.0, 0.0).astype(jnp.float32)
            found.append((tile, block_cells(data_ref, row, step, scale)))
        for tile, cells in found:
            for a in range(2):
                for l in range(TZ):
                    start = (a * 512 + tile * TZ + l) * depth
                    rows = pl.ds(pl.multiple_of(start, 8), TX)
                    part = (a * TZ + l) * TX
                    grid_ref[rows, :] += cells[part : part + TX]
        return carry if after is None else after((n + 1) * size, carry)

    return lax.fori_loop(0, (held + size - 1) // size, group, 0)


def direct(list_ref):
    def find(i):
        code = list_ref[LISTED + i]
        row = lax.shift_right_logical(code, 7)
        return row, (row & 112) + (code & 15)

    return find


def listed(row_ref, tile_ref):
    return lambda i: (row_ref[i], tile_ref[i])


def list_headed(head_ref, row_ref, tile_ref, room, base):
    def source(g, total):
        def entry(i, at):
            row_ref[at] = g * (5 * room + 8) + i
            tile_ref[at] = head_ref[g, i] + base * g
            return at + 1

        return lax.fori_loop(0, head_ref[g, LAST], entry, total)

    return lax.fori_loop(0, 8, source, 0)


def clear_grid(grid_ref):
    def clear(i, carry):
        grid_ref[pl.ds(pl.multiple_of(i * 64, 64), 64), :] = jnp.zeros((64, CAP), jnp.float32)
        return carry

    lax.fori_loop(0, 16384 // 64, clear, 0, unroll=4)


def list_strays(head_ref, row_ref, tile_ref, ends_ref, next_ref):
    for h in range(8):
        next_ref[h] = 0

    def slab(g, total):
        def source(h, so_far):
            held = head_ref[h, LAST]

            def more(state):
                i, _ = state
                return (i < held) & (lax.shift_right_logical(head_ref[h, i & 63], 4) == g)

            def entry(state):
                i, at = state
                row_ref[at] = h * ROWS_S + i
                tile_ref[at] = head_ref[h, i]
                return i + 1, at + 1

            i, so_far = lax.while_loop(more, entry, (next_ref[h], so_far))
            next_ref[h] = i
            return so_far

        total = lax.fori_loop(0, 8, source, total)
        ends_ref[g] = total
        return total

    return lax.fori_loop(0, 8, slab, 0)


def spread_direct(list_ref, data_ref, out_ref, grid_ref, sem):
    clear_grid(grid_ref)

    def outward(a, slab):
        rows = pl.ds(pl.multiple_of(a * 8192 + slab * 1024, 1024), 1024)
        return pltpu.make_async_copy(grid_ref.at[rows], out_ref.at[rows], sem.at[a, slab])

    def leave(slab):
        for a in range(2):
            outward(a, slab).start()
        return slab + 1

    def after(done, slab):
        return lax.while_loop(
            lambda at: (at < 8) & (list_ref[2 + jnp.minimum(at, 7)] <= done), leave, slab
        )

    slab = add_listed(
        direct(list_ref), list_ref[0], SLOTS, data_ref, grid_ref, TX, GROUP, after=after
    )
    lax.while_loop(lambda at: at < 8, leave, slab)
    for slab in range(8):
        for a in range(2):
            outward(a, slab).wait()


def spread_round(head_ref, data_ref, from_ref, grid_ref, row_ref, tile_ref, sem):
    copy = pltpu.make_async_copy(from_ref, grid_ref, sem)
    copy.start()
    copy.wait()
    held = list_headed(head_ref, row_ref, tile_ref, ROOM, 16)
    add_listed(listed(row_ref, tile_ref), held, ROOM, data_ref, grid_ref, TX, GROUP)


def quarters(re, im):
    s02r, s02i = re[0] + re[2], im[0] + im[2]
    d02r, d02i = re[0] - re[2], im[0] - im[2]
    s13r, s13i = re[1] + re[3], im[1] + im[3]
    d13r, d13i = re[1] - re[3], im[1] - im[3]
    return [
        (s02r + s13r, s02i + s13i),
        (d02r - d13i, d02i + d13r),
        (s02r - s13r, s02i - s13i),
        (d02r + d13i, d02i - d13r),
    ]


def three_pass(high, low, value):
    top, rest = halves(value)

    def dot(a, b):
        return jnp.dot(a, b, preferred_element_type=jnp.float32)

    return (dot(high, top) + dot(high, rest)) + dot(low, top)


def spread_and_turn(
    list_ref, head_ref, data_ref, high_ref, low_ref, from_ref, out_ref,
    grid_ref, sent_ref, row_ref, tile_ref, ends_ref, next_ref, sem, out_sem,
):
    def inward(a, slab):
        rows = pl.ds(pl.multiple_of(a * 512 + slab * 64, 64), 64)
        return pltpu.make_async_copy(
            from_ref.at[rows], grid_ref.at[rows, pl.ds(0, TX), :], sem.at[a, slab]
        )

    def arrive(slab):
        for a in range(2):
            inward(a, slab).wait()
        return slab + 1

    for slab in range(8):
        for a in range(2):
            inward(a, slab).start()
    held = list_strays(head_ref, row_ref, tile_ref, ends_ref, next_ref)
    flat = grid_ref.reshape(1024 * DEPTH, CAP)
    sent = sent_ref.reshape(128 * WIDE, CAP)

    def before(need, slab):
        return lax.while_loop(
            lambda at: (at < 8) & ((at == 0) | (ends_ref[jnp.maximum(at - 1, 0)] < need)),
            arrive,
            slab,
        )

    slab = add_listed(
        listed(row_ref, tile_ref), held, STRAYS, data_ref, flat, DEPTH, GROUP, before=before
    )
    lax.while_loop(lambda at: at < 8, arrive, slab)

    def columns(n, carry):
        j = 2 * n

        def plane(a, q):
            return jnp.concatenate(
                [
                    flat[pl.ds((a * 512 + q * 128) * DEPTH + j + u, 128, stride=DEPTH), :]
                    for u in range(2)
                ],
                axis=1,
            )

        re = [plane(0, q) for q in range(4)]
        im = [plane(1, q) for q in range(4)]
        for r, (real, imag) in enumerate(quarters(re, im)):
            turned = three_pass(high_ref[r], low_ref[r], jnp.concatenate([real, imag], axis=0))
            for a in range(2):
                for u in range(2):
                    sent[pl.ds(r * 32 + a * 16 + j + u, 128, stride=WIDE), :] = turned[
                        a * 128 : (a + 1) * 128, u * 128 : (u + 1) * 128
                    ]
        return carry

    def outward(n):
        return pltpu.make_async_copy(sent_ref.at[:, n], out_ref.at[:, n], out_sem.at[n])

    lax.fori_loop(0, 4, columns, 0, unroll=4)

    @pl.when(list_ref[1] > 0)
    def _():
        sent[pl.ds(0, 128, stride=WIDE), :] = jnp.full((128, CAP), MARK, jnp.float32)

    for n in range(8):
        outward(2 * n).start()
    lax.fori_loop(4, 8, columns, 0, unroll=4)
    for n in range(8):
        outward(2 * n + 1).start()
    for n in range(16):
        outward(n).wait()


def turn_planes(data_ref, high_ref, low_ref, y_ref, out_ref, mark_ref, rows_ref):
    @pl.when(pl.program_id(0) == 0)
    def _():
        most = data_ref[0, 0, :, 0, 0, 0]
        for n in range(1, 16):
            most = jnp.maximum(most, data_ref[n // 4, n % 4, :, 0, 0, 0])
        mark_ref[0] = (jnp.max(most) > 0.1 * MARK).astype(jnp.int32)

    def plane(c, bx, by):
        return data_ref[bx, by, :, 0, c].reshape(128, CAP)

    for pair in range(2):
        ys = (2 * pair, 2 * pair + 1)
        re = [jnp.concatenate([plane(0, bx, by) for by in ys], axis=1) for bx in range(4)]
        im = [jnp.concatenate([plane(1, bx, by) for by in ys], axis=1) for bx in range(4)]
        for r, (real, imag) in enumerate(quarters(re, im)):
            turned = three_pass(high_ref[r], low_ref[r], jnp.concatenate([real, imag], axis=0))
            for a in range(2):
                for u in range(2):
                    start = (a * 4 + ys[u]) * GRID + r
                    rows_ref[pl.ds(start, 128, stride=4), :] = turned[
                        a * 128 : (a + 1) * 128, u * 128 : (u + 1) * 128
                    ]
    left = jnp.concatenate(
        [rows_ref[n * GRID : (n + 1) * GRID, :].astype(jnp.bfloat16) for n in range(8)], axis=1
    )
    for n in range(4):
        out_ref[n // 2, 0, :, (n % 2) * 256 : (n % 2 + 1) * 256] = jnp.dot(
            left, y_ref[:, n * 256 : (n + 1) * 256], preferred_element_type=jnp.float32
        )


def smem():
    return pl.BlockSpec(memory_space=pltpu.SMEM)


def vmem():
    return pl.BlockSpec(memory_space=pltpu.VMEM)


def params(name):
    return pltpu.CompilerParams(vmem_limit_bytes=VMEM_MIB.get(name, 40) * MIB)


def swap(array, axis):
    return lax.all_to_all(array, axis, split_axis=0, concat_axis=0, tiled=True)


def call(kernel, out_shape, in_specs, out_specs, **options):
    return pl.pallas_call(
        kernel,
        out_shape=out_shape,
        in_specs=in_specs,
        out_specs=out_specs,
        compiler_params=params(kernel.__name__),
        name=kernel.__name__,
        **options,
    )


def anywhere():
    return pl.BlockSpec(memory_space=pl.ANY)


def large():
    return pl.BlockSpec(memory_space=pl.ANY)


def rows_of(rows):
    return jax.ShapeDtypeStruct((rows, CAP), jnp.float32)


def ints(count):
    return jax.ShapeDtypeStruct((count,), jnp.int32)


def body(z_high, z_low, x_high, x_low, y_table, spots, values, dest_brick, dest_tile, live_count):
    points = (
        dest_brick.reshape(256),
        dest_tile[0],
        live_count[0],
        spots[0].transpose(1, 0, 2),
        values[0],
    )

    def finish(blocks, heads, data, grid):
        columns = call(
            spread_and_turn,
            jax.ShapeDtypeStruct((128, 16, 8, CAP), jnp.float32),
            [smem(), smem(), vmem(), vmem(), vmem(), anywhere()],
            large(),
            scratch_shapes=[
                pltpu.VMEM((1024, DEPTH, CAP), jnp.float32),
                pltpu.VMEM((128, WIDE // 8, 8, CAP), jnp.float32),
                *[pltpu.SMEM((n,), jnp.int32) for n in (8 * STRAYS, 8 * STRAYS, 8, 8)],
                pltpu.SemaphoreType.DMA((2, 8)),
                pltpu.SemaphoreType.DMA((16,)),
            ],
        )(blocks, heads, data, z_high, z_low, grid.reshape(1024, TX, CAP))
        planes = swap(columns.reshape(128, 4, 2, TX, CAP), AXES).reshape(4, 4, 8, 4, 2, TX, CAP)
        return call(
            turn_planes,
            (jax.ShapeDtypeStruct((2, 4, GRID, GRID), jnp.float32), ints(1)),
            [
                pl.BlockSpec((4, 4, 8, 1, 2, TX, CAP), lambda q: (0, 0, 0, q, 0, 0, 0)),
                vmem(),
                vmem(),
                vmem(),
            ],
            (pl.BlockSpec((2, 1, GRID, GRID), lambda q: (0, q, 0, 0)), smem()),
            grid=(4,),
            scratch_shapes=[pltpu.VMEM((8 * GRID, CAP), jnp.float32)],
        )(planes, x_high, x_low, y_table)

    me = lax.axis_index("gz").astype(jnp.int32).reshape(1)
    sent = call(
        pack_blocks,
        rows_of(128 * 16),
        [smem()] * 4 + [vmem()] * 2,
        vmem(),
        scratch_shapes=[pltpu.SMEM((n,), jnp.int32) for n in (256, 264, 128, 16)],
    )(me, *points)
    held = swap(sent.reshape(128, 16, CAP), AXES)
    heads = held[:, 15, :SLOTS].astype(jnp.int32).reshape(128 * SLOTS)
    held = held.reshape(128 * 16, CAP)
    strays, blocks = call(
        sort_blocks,
        (rows_of(8 * ROWS_S), ints(LIST)),
        [smem(), smem(), vmem()],
        (vmem(), smem()),
        scratch_shapes=[pltpu.SMEM((8,), jnp.int32)],
    )(me, heads, held)
    strays = swap(strays.reshape(8, ROWS_S, CAP), "gz")
    grid = call(
        spread_direct,
        rows_of(16384),
        [smem(), vmem()],
        large(),
        scratch_shapes=[pltpu.VMEM((16384, CAP), jnp.float32), pltpu.SemaphoreType.DMA((2, 8))],
        cost_estimate=pl.CostEstimate(flops=3 * 10**10, bytes_accessed=10**8, transcendentals=0),
    )(blocks, held)
    stray_heads = strays[:, 5 * STRAYS].astype(jnp.int32)
    density, mark = finish(blocks, stray_heads, strays.reshape(8 * ROWS_S, CAP), grid)

    def general(state):
        _, again, *given = lax.optimization_barrier((*state, *points))
        parts = call(
            pack_bricks,
            rows_of(16 * ROWS1),
            [smem()] * 3 + [vmem()] * 2,
            vmem(),
            scratch_shapes=[pltpu.SMEM((16,), jnp.int32)],
        )(*given)
        parts = swap(parts.reshape(16, ROWS1, CAP), "brick")
        head = parts[:, 5 * PER_DEST].astype(jnp.int32)
        parts = parts.reshape(16 * ROWS1, CAP)

        def another(inner):
            turn, _, total = inner
            packed = call(
                pack_tiles,
                rows_of(8 * ROWS2),
                [smem(), smem(), vmem()],
                vmem(),
                scratch_shapes=[pltpu.SMEM((8,), jnp.int32)],
            )(turn, head, parts)
            blocks = swap(packed.reshape(8, ROWS2, CAP), "gz")
            told = blocks[:, 5 * ROOM : 5 * ROOM + 2].astype(jnp.int32)
            total = call(
                spread_round,
                rows_of(16384),
                [smem(), vmem(), anywhere()],
                vmem(),
                scratch_shapes=[
                    pltpu.SMEM((8 * ROOM,), jnp.int32),
                    pltpu.SMEM((8 * ROOM,), jnp.int32),
                    pltpu.SemaphoreType.DMA,
                ],
            )(told[:, 0], blocks.reshape(8 * ROWS2, CAP), total)
            return turn + 1, ((jnp.max(told[:, 1]) + ROOM - 1) // ROOM).reshape(1), total

        _, _, total = lax.while_loop(
            lambda inner: inner[0][0] < inner[1][0],
            another,
            (
                jnp.zeros((1,), jnp.int32),
                jnp.ones((1,), jnp.int32),
                jnp.zeros((16384, CAP), jnp.float32),
            ),
        )
        none = jnp.zeros((8, CAP), jnp.int32)
        return finish(
            jnp.zeros((LIST,), jnp.int32),
            none,
            jnp.zeros((8 * ROWS_S, CAP), jnp.float32),
            total,
        )

    density, _ = lax.while_loop(lambda state: state[1][0] > 0, general, (density, mark))
    return density


def solution(mesh):
    in_specs = (
        P("gz", "brick", None, None),
        P("gz", "brick", None, None),
        P("gz", "brick", None),
        P("gz", "brick"),
        P("gz", "brick"),
    )
    out_specs = P(None, AXES, None, None)
    inverse = 1.0 / correction_of(GRID)
    z_high, z_low = quarter_tables(inverse * GRID ** (-1.5))
    x_high, x_low = quarter_tables(inverse)
    y_table = full_table(inverse)

    def whole(*args):
        tables = [jnp.asarray(t) for t in (z_high, z_low, x_high, x_low, y_table)]
        return jax.shard_map(
            functools.partial(body),
            mesh=mesh,
            in_specs=(P(),) * 5 + in_specs,
            out_specs=out_specs,
            check_vma=False,
        )(*tables, *args)

    return whole
```
